32 devices in a mesh: dp: 8 (over z, x), tensor: 4 (over y, core).
Axes of the slice: x: 2, y: 2, z: 4, core: 2. Of those that a mesh axis runs over, the one named last changes fastest.
Arguments:
- tokens: bfloat16 [6144, 2048], P(('dp', 'tensor')), may hold values from -6 to 6
- query_weight: float32 [2048, 2048], P('dp', 'tensor'), may hold values from -0.125 to 0.125
- key_weight: float32 [2048, 256], P('dp', 'tensor'), may hold values from -0.125 to 0.125
- value_weight: float32 [2048, 256], P('dp', 'tensor'), may hold values from -0.125 to 0.125
- output_weight: float32 [2048, 2048], P('tensor', 'dp'), may hold values from -0.375 to 0.375
- gate_weight: float32 [2048, 5632], P('dp', 'tensor'), may hold values from -0.125 to 0.125
- up_weight: float32 [2048, 5632], P('dp', 'tensor'), may hold values from -0.125 to 0.125
- down_weight: float32 [5632, 2048], P('tensor', 'dp'), may hold values from -0.078125 to 0.078125
- attention_gain: float32 [2048], P('dp'), may hold values from 0.5 to 1.5
- feed_gain: float32 [2048], P('dp'), may hold values from 0.5 to 1.5
- doc_lengths: int32 [8, 6], P('dp'), may hold values from 0 to 614, as said below
- cotangent: bfloat16 [6144, 2048], P(('dp', 'tensor')), may hold values from -6 to 6
Outputs:
- layer_out: bfloat16 [6144, 2048], P(('dp', 'tensor'))
- input_grad: float32 [6144, 2048], P(('dp', 'tensor'))
- query_grad: float32 [2048, 2048], P('dp', 'tensor')
- key_grad: float32 [2048, 256], P('dp', 'tensor')
- value_grad: float32 [2048, 256], P('dp', 'tensor')
- output_grad: float32 [2048, 2048], P('tensor', 'dp')
- gate_grad: float32 [2048, 5632], P('dp', 'tensor')
- up_grad: float32 [2048, 5632], P('dp', 'tensor')
- down_grad: float32 [5632, 2048], P('tensor', 'dp')
- attention_gain_grad: float32 [2048], P('dp')
- feed_gain_grad: float32 [2048], P('dp')
The draws below stay inside these ranges and needn't reach their ends.
Inputs may be any that keep to these rules, and one draw needn't show every extreme that they name: `doc_lengths`: entry 1 of every row is exactly 614; entry 0 is at most (154) // 2, every later entry at most (154) // 8, so that a row sums to at most 768.
All inputs are finite; a program needn't handle non-finite values.
Results may differ from the reference program's by a relative error of at most 0.025.
Values may be sent and summed in bfloat16 or wider, within the bound.
No kernel may reach another device: no remote copies, remote signals or barrier semaphores. Data moves between devices by JAX's collectives and lax.ppermute only.
A program may use at most 192 MiB of HBM per device.

```python
import math
import jax
import jax.numpy as jnp
from jax import lax

D = 2048
HEADS = 32
KV_HEADS = 4
HEAD_DIM = 64
FF = 5632
SEGS = 6
TOK_GRP = 768
LONG = 614
GROUPS = 8
TOKENS = 6144
N_TENSOR = 4


def draw_doc_lengths(key, part):
    key = jax.random.fold_in(key, 7)
    spare = TOK_GRP - LONG
    first_key, rest_key = jax.random.split(key)
    before = jax.random.randint(first_key, (GROUPS, 1), 0, spare // 2 + 1)
    after = jax.random.randint(rest_key, (GROUPS, SEGS - 2), 0, spare // (2 * (SEGS - 2)) + 1)
    whole = jnp.full((GROUPS, 1), LONG, jnp.int32)
    return jnp.concatenate([before.astype(jnp.int32), whole, after.astype(jnp.int32)], axis=1)


def spiked(drawn, rng, source, target, blocks, factor):
    def block_of(dim):
        return (jnp.arange(drawn.shape[dim]) // (drawn.shape[dim] // blocks)).reshape((-1,) + (1,) * (drawn.ndim - 1 - dim))

    first = jax.random.permutation(rng, blocks)[block_of(target)]
    far = (block_of(target) + blocks // 2) % blocks
    return jnp.where((block_of(source) == first) | (block_of(source) == far), factor * drawn, drawn)


def shard_levels(own_key, shape, cuts, low, top_value):
    def one(dim, blocks):
        steps = jax.random.uniform(jax.random.fold_in(jax.random.fold_in(own_key, 6), dim), (blocks,), jnp.float32, low / len(cuts), top_value / len(cuts))
        return jnp.repeat(jnp.exp(steps), shape[dim] // blocks).reshape((-1,) + (1,) * (len(shape) - dim - 1))

    loudness = one(*cuts[0])
    for cut in cuts[1:]:
        loudness = loudness * one(*cut)
    return loudness


def normal_values(key, extent, scale, most, cuts=(), held_as=jnp.bfloat16):
    drawn = jax.random.normal(key, extent, jnp.float32) * scale
    if len(cuts) > 0:
        drawn = shard_levels(key, extent, cuts, -0.22, 0.18) * drawn
    return jnp.clip(drawn, min=-most, max=most).astype(held_as)


def bell_draw_with(rng, shape, width, bound, pieces, heavy, kind=jnp.bfloat16):
    values = width * jax.random.normal(rng, shape, jnp.float32)
    if pieces:
        values = values * shard_levels(rng, shape, pieces, -0.22, 0.18)
    return jnp.clip(spiked(values, jax.random.fold_in(rng, 3), *heavy), -bound, bound).astype(kind)


def setup_inputs(seed: int = 0) -> dict:
    arg_keys = jax.random.split(jax.random.key(seed), 13)
    return {
        "tokens": bell_draw_with(arg_keys[0], (TOKENS, D), 1.0, 6.0, ((0, 32),), (0, 1, 32, 2.75)),
        "query_weight": normal_values(arg_keys[1], (D, HEADS * HEAD_DIM), D ** -0.5, 0.125, ((0, 8), (1, 4)), jnp.float32),
        "key_weight": normal_values(arg_keys[2], (D, KV_HEADS * HEAD_DIM), D ** -0.5, 0.125, ((0, 8), (1, 4)), jnp.float32),
        "value_weight": normal_values(arg_keys[3], (D, KV_HEADS * HEAD_DIM), D ** -0.5, 0.125, ((0, 8), (1, 4)), jnp.float32),
        "output_weight": normal_values(arg_keys[4], (HEADS * HEAD_DIM, D), (HEADS * HEAD_DIM // 8) ** -0.5, 0.375, ((0, 4), (1, 8)), jnp.float32),
        "gate_weight": normal_values(arg_keys[5], (D, FF), D ** -0.5, 0.125, ((0, 8), (1, 4)), jnp.float32),
        "up_weight": normal_values(arg_keys[6], (D, FF), D ** -0.5, 0.125, ((0, 8), (1, 4)), jnp.float32),
        "down_weight": normal_values(arg_keys[7], (FF, D), FF ** -0.5, 0.078125, ((0, 4), (1, 8)), jnp.float32),
        "attention_gain": jnp.clip(1.0 + 0.1 * jax.random.normal(arg_keys[8], (D,), jnp.float32), 0.5, 1.5),
        "feed_gain": jnp.clip(1.0 + 0.1 * jax.random.normal(arg_keys[9], (D,), jnp.float32), 0.5, 1.5),
        "doc_lengths": draw_doc_lengths(jax.random.fold_in(arg_keys[12], 71), 0),
        "cotangent": bell_draw_with(arg_keys[11], (TOKENS, D), 1.0, 6.0, ((0, 32),), (0, 1, 32, 2.75)),
    }


EPS = 1e-05
NEG = -1e+30

@jax.custom_vjp
def low(v):
    return lax.optimization_barrier(v.astype(jnp.bfloat16)).astype(jnp.float32)

@jax.custom_vjp
def low_back(v):
    return v

def low_keep(v):
    return (low(v), None)

def low_pass(kept, grad):
    return (grad,)

def back_keep(v):
    return (v, None)

def back_low(kept, grad):
    return (low(grad),)
low.defvjp(low_keep, low_pass)
low_back.defvjp(back_keep, back_low)

def group_layout(counts, total):
    ends = jnp.cumsum(counts).astype(jnp.int32)
    starts = (ends - counts).astype(jnp.int32)
    place = jnp.arange(total, dtype=jnp.int32)
    segment = lax.optimization_barrier(jnp.sum((place[:, None] >= ends[None, :]).astype(jnp.int32), axis=1))
    bounds = jnp.concatenate([starts, ends[-1:]]).astype(jnp.int32)
    slots = jnp.arange(bounds.shape[0], dtype=jnp.int32)
    begin = lax.optimization_barrier(jnp.sum(jnp.where(segment[:, None] == slots[None, :], bounds[None, :], 0), axis=1))
    position = (place - begin).astype(jnp.float32)
    valid = (place < ends[-1]).astype(jnp.float32)
    allowed = (segment[:, None] == segment[None, :]) & (place[None, :] <= place[:, None])
    return (position, valid, allowed)

def angle_tables(position):
    half = HEAD_DIM // 2
    freq = jnp.exp(jnp.arange(half, dtype=jnp.float32) * (-2.0 * math.log(10000.0) / HEAD_DIM))
    angle = position[:, None] * freq[None, :]
    return (jnp.cos(angle), jnp.sin(angle))

def rotate(values, cosine, sine, sign):
    rows = values.shape[0]
    split = values.reshape(rows, -1, HEAD_DIM)
    half = HEAD_DIM // 2
    first = split[..., :half]
    second = split[..., half:]
    cos_three = cosine[:, None, :]
    sin_three = sign * sine[:, None, :]
    turned = jnp.concatenate([first * cos_three - second * sin_three, second * cos_three + first * sin_three], axis=-1)
    return turned.reshape(rows, -1)

def matmul(left, right):
    return jnp.dot(left, right, precision=lax.Precision.HIGHEST)

def rms_scale(values):
    return lax.rsqrt(lax.optimization_barrier(jnp.mean(values * values, axis=1, keepdims=True)) + EPS)

def group_forward(resid, counts, weights):
    query_w, key_w, value_w, output_w, gate_w, up_w, down_w, gain_one, gain_two = weights
    total = resid.shape[0]
    groups_tp = N_TENSOR
    query_cols = HEADS * HEAD_DIM // groups_tp
    kv_cols = KV_HEADS * HEAD_DIM // groups_tp
    unit_cols = FF // groups_tp
    position, valid, allowed = group_layout(counts, total)
    cosine, sine = angle_tables(position)
    normed_one = low(resid * rms_scale(resid) * gain_one)
    query_parts = []
    key_parts = []
    value_parts = []
    for member in range(groups_tp):
        shared = low_back(normed_one)
        query_parts.append(low_back(matmul(shared, query_w[:, member * query_cols:(member + 1) * query_cols])))
        key_parts.append(low_back(matmul(shared, key_w[:, member * kv_cols:(member + 1) * kv_cols])))
        value_parts.append(low_back(matmul(shared, value_w[:, member * kv_cols:(member + 1) * kv_cols])))
    queries = low(rotate(jnp.concatenate(query_parts, axis=1), cosine, sine, 1.0))
    keys = low(rotate(jnp.concatenate(key_parts, axis=1), cosine, sine, 1.0))
    values = low(jnp.concatenate(value_parts, axis=1))
    per_kv = HEADS // KV_HEADS
    query_heads = queries.reshape(total, KV_HEADS, per_kv, HEAD_DIM).transpose(1, 2, 0, 3)
    key_heads = keys.reshape(total, KV_HEADS, HEAD_DIM).transpose(1, 0, 2)
    value_heads = values.reshape(total, KV_HEADS, HEAD_DIM).transpose(1, 0, 2)

    def attend(items):
        query_block, key_block, value_block = items
        scores = low_back(HEAD_DIM ** (-0.5) * jnp.einsum('gqd,kd->gqk', query_block, key_block, precision=lax.Precision.HIGHEST))
        scores = jnp.where(allowed[None], scores, NEG)
        probs = low(jax.nn.softmax(scores, axis=-1))
        return jnp.einsum('gqk,kd->gqd', probs, value_block, precision=lax.Precision.HIGHEST)
    mixed = lax.map(jax.checkpoint(attend), (query_heads, key_heads, value_heads))
    mixed = mixed.transpose(2, 0, 1, 3).reshape(total, HEADS * HEAD_DIM)
    attended = low(low_back(mixed * valid[:, None]))
    attn_total = jnp.zeros((total, D), jnp.float32)
    for member in range(groups_tp):
        attn_total = attn_total + low(matmul(attended[:, member * query_cols:(member + 1) * query_cols], output_w[member * query_cols:(member + 1) * query_cols, :]))
    middle = resid + low_back(attn_total)
    normed_two = low(middle * rms_scale(middle) * gain_two)
    gate_parts = []
    upper_parts = []
    for member in range(groups_tp):
        shared = low_back(normed_two)
        gate_parts.append(low_back(matmul(shared, gate_w[:, member * unit_cols:(member + 1) * unit_cols])))
        upper_parts.append(low_back(matmul(shared, up_w[:, member * unit_cols:(member + 1) * unit_cols])))
    gate = jnp.concatenate(gate_parts, axis=1)
    upper = jnp.concatenate(upper_parts, axis=1)
    hidden = low(jax.nn.silu(gate) * upper)
    feed_total = jnp.zeros((total, D), jnp.float32)
    for member in range(groups_tp):
        feed_total = feed_total + low(matmul(hidden[:, member * unit_cols:(member + 1) * unit_cols], down_w[member * unit_cols:(member + 1) * unit_cols, :]))
    return middle + low_back(feed_total)

def reference(tokens, query_weight, key_weight, value_weight, output_weight, gate_weight, up_weight, down_weight, attention_gain, feed_gain, doc_lengths, cotangent):
    groups = tokens.shape[0] // TOK_GRP

    def forward(resid, query_w, key_w, value_w, output_w, gate_w, up_w, down_w, gain_one, gain_two):
        weights = (low(query_w), low(key_w), low(value_w), low(output_w), low(gate_w), low(up_w), low(down_w), low(gain_one), low(gain_two))
        stacked = resid.reshape(groups, TOK_GRP, D)
        checked = jax.checkpoint(group_forward)

        def step(carry, item):
            return (carry, checked(item[0], item[1], weights))
        _, outputs = lax.scan(step, jnp.zeros((), jnp.float32), (stacked, doc_lengths))
        return outputs.reshape(groups * TOK_GRP, D)
    result, pullback = jax.vjp(forward, tokens.astype(jnp.float32), query_weight, key_weight, value_weight, output_weight, gate_weight, up_weight, down_weight, attention_gain, feed_gain)
    grads = pullback(cotangent.astype(jnp.float32))
    return (result.astype(jnp.bfloat16), grads[0], grads[1], grads[2], grads[3], grads[4], grads[5], grads[6], grads[7], grads[8], grads[9])
```

```python
import math

import jax
import jax.numpy as jnp
from jax import lax
from jax.sharding import PartitionSpec as P

HEAD_DIM = 64


EPS = 1e-05
NEG = -1e30
HALF = jnp.bfloat16
FULL = jnp.float32


def group_layout(counts, total):
    ends = jnp.cumsum(counts)
    starts = ends - counts
    place = jnp.arange(total, dtype=jnp.int32)
    segment = jnp.sum((place[:, None] >= ends[None, :]).astype(jnp.int32), axis=1)
    bounds = jnp.concatenate([starts, ends[-1:]])
    slots = jnp.arange(bounds.shape[0], dtype=jnp.int32)
    begin = jnp.sum(jnp.where(segment[:, None] == slots[None, :], bounds[None, :], 0), axis=1)
    position = (place - begin).astype(FULL)
    valid = (place < ends[-1]).astype(FULL)
    allowed = (segment[:, None] == segment[None, :]) & (place[None, :] <= place[:, None])
    return (position, valid, allowed)


def angle_tables(position):
    half = HEAD_DIM // 2
    freq = jnp.exp(jnp.arange(half, dtype=FULL) * (-2.0 * math.log(10000.0) / HEAD_DIM))
    angle = position[:, None] * freq[None, :]
    return (jnp.cos(angle), jnp.sin(angle))


def rotate(values, cosine, sine, sign):
    rows = values.shape[0]
    split = values.reshape(rows, -1, HEAD_DIM)
    half = HEAD_DIM // 2
    first = split[..., :half]
    second = split[..., half:]
    cos_three = cosine[:, None, :]
    sin_three = sign * sine[:, None, :]
    turned = jnp.concatenate(
        [first * cos_three - second * sin_three, second * cos_three + first * sin_three], axis=-1
    )
    return turned.reshape(rows, -1)


def contract_rows(left, right):
    return lax.dot_general(left, right, (((0,), (0,)), ((), ())), preferred_element_type=FULL)


def contract_cols(left, right):
    return lax.dot_general(left, right, (((1,), (1,)), ((), ())), preferred_element_type=FULL)


def product(left, right):
    return jnp.dot(left, right, preferred_element_type=FULL)


def rms_scale(values):
    return lax.rsqrt(jnp.mean(values * values, axis=1, keepdims=True) + EPS)


def ring_order(count):
    return list(range(0, count, 2)) + list(range(count - 1, 0, -2))


class Ring:
    def __init__(self, count):
        self.count = count
        self.half = count // 2
        self.order = ring_order(count)
        self.up = [(self.order[i], self.order[(i + 1) % count]) for i in range(count)]
        self.down = [(b, a) for a, b in self.up]
        place = [0] * count
        for spot, member in enumerate(self.order):
            place[member] = spot
        here = jnp.asarray(place, jnp.int32)[lax.axis_index("dp")]
        self.offsets = [0]
        for step in range(1, self.half):
            self.offsets += [-step, step]
        self.offsets.append(self.half)
        order = jnp.asarray(self.order, jnp.int32)
        self.members = [order[(here + offset) % count] for offset in self.offsets]

    def shuffle(self, values):
        width = values.shape[1] // self.count
        return jnp.concatenate(
            [lax.dynamic_slice_in_dim(values, m * width, width, 1) for m in self.members], axis=1
        )

    def unshuffle(self, values):
        width = values.shape[1] // self.count
        out = jnp.zeros_like(values)
        for slot, member in enumerate(self.members):
            piece = values[:, slot * width : (slot + 1) * width]
            out = lax.dynamic_update_slice_in_dim(out, piece, member * width, 1)
        return out

    def gather(self, shard):
        blocks = [shard]
        above = below = shard
        for _ in range(1, self.half):
            above = lax.ppermute(above, "dp", self.up)
            below = lax.ppermute(below, "dp", self.down)
            blocks += [above, below]
        cut = shard.shape[0] // 2
        upper = lax.ppermute(above[:cut], "dp", self.up)
        lower = lax.ppermute(below[cut:], "dp", self.down)
        blocks.append(jnp.concatenate([upper, lower], axis=0))
        return blocks

    def reduce(self, part):
        far = part(self.count - 1)
        cut = far.shape[0] // 2
        above = lax.ppermute(far[:cut].astype(HALF), "dp", self.up).astype(FULL)
        below = lax.ppermute(far[cut:].astype(HALF), "dp", self.down).astype(FULL)
        for step in range(self.half - 1, 0, -1):
            top = part(2 * step)
            low = part(2 * step - 1)
            if step == self.half - 1:
                top = jnp.concatenate([top[:cut] + above, top[cut:]], axis=0)
                low = jnp.concatenate([low[:cut], low[cut:] + below], axis=0)
            else:
                top = top + above
                low = low + below
            above = lax.ppermute(top.astype(HALF), "dp", self.up).astype(FULL)
            below = lax.ppermute(low.astype(HALF), "dp", self.down).astype(FULL)
        return part(0) + above + below


def beside(index):
    return [(i, i ^ index) for i in range(4)]


def gather_rows(rows):
    mine = lax.axis_index("tensor")
    count = rows.shape[0]
    first = lax.ppermute(rows, "tensor", beside(2))
    pieces = (
        (0, rows),
        (1, lax.ppermute(rows, "tensor", beside(1))),
        (2, first),
        (3, lax.ppermute(first, "tensor", beside(1))),
    )
    out = jnp.zeros((4 * count, rows.shape[1]), rows.dtype)
    for index, piece in pieces:
        out = lax.dynamic_update_slice_in_dim(out, piece, (mine ^ index) * count, 0)
    return out


def scatter_rows(values):
    mine = lax.axis_index("tensor")
    values = values.astype(HALF)
    count = values.shape[0] // 4

    def piece(index):
        return lax.dynamic_slice_in_dim(values, (mine ^ index) * count, count, 0)

    across = lax.ppermute(piece(3), "tensor", beside(1)).astype(FULL)
    near = lax.ppermute(piece(1), "tensor", beside(1)).astype(FULL)
    send = (piece(2).astype(FULL) + across).astype(HALF)
    far = lax.ppermute(send, "tensor", beside(2)).astype(FULL)
    return piece(0).astype(FULL) + near + far


def per_device(
    tokens,
    query_weight,
    key_weight,
    value_weight,
    output_weight,
    gate_weight,
    up_weight,
    down_weight,
    attention_gain,
    feed_gain,
    doc_lengths,
    cotangent,
):
    ring = Ring(lax.axis_size("dp"))
    own_rows, width = tokens.shape
    block = query_weight.shape[0]
    tokens = ring.shuffle(tokens)
    cotangent = ring.shuffle(cotangent)

    inner = query_weight.shape[1]
    kv_width = key_weight.shape[1]
    gains = jnp.stack([attention_gain, feed_gain]).astype(HALF)
    gains = jnp.pad(gains, ((0, 30), (0, inner + 2 * kv_width - block)))
    first_shard = jnp.concatenate(
        [
            jnp.concatenate([query_weight, key_weight, value_weight], axis=1).astype(HALF),
            gains,
        ],
        axis=0,
    )
    first_blocks = ring.gather(first_shard)
    first_copy = jnp.concatenate([b[:block] for b in first_blocks], axis=0)
    gain_one = jnp.concatenate([b[block, :block] for b in first_blocks]).astype(FULL)
    gain_two = jnp.concatenate([b[block + 1, :block] for b in first_blocks]).astype(FULL)
    output_copy = jnp.concatenate(ring.gather(output_weight.astype(HALF)), axis=1)
    gate_copy = jnp.concatenate(ring.gather(gate_weight.astype(HALF)), axis=0)
    up_copy = jnp.concatenate(ring.gather(up_weight.astype(HALF)), axis=0)
    down_copy = jnp.concatenate(ring.gather(down_weight.astype(HALF)), axis=1)

    total = own_rows * lax.axis_size("tensor")
    position, valid, allowed = group_layout(doc_lengths[0], total)
    cosine, sine = angle_tables(position)
    head_dim = HEAD_DIM
    local_heads = inner // head_dim
    scale = head_dim ** (-0.5)
    resid = tokens.astype(FULL)
    scale_one = rms_scale(resid)
    rows_in = gather_rows(tokens).astype(FULL)
    rows_one = (rows_in * rms_scale(rows_in) * gain_one).astype(HALF)
    joined = product(rows_one, first_copy)
    queries = rotate(joined[:, :inner], cosine, sine, 1.0).astype(HALF)
    keys = rotate(joined[:, inner : inner + kv_width], cosine, sine, 1.0).astype(HALF)
    values = joined[:, inner + kv_width :].astype(HALF)

    def head_scores(head):
        query_head = lax.dynamic_slice_in_dim(queries, head * head_dim, head_dim, 1)
        scores = jnp.where(allowed, scale * contract_cols(query_head, keys), NEG)
        return (query_head, scores)

    def forward_head(head, carry):
        mixed, logsum = carry
        _, scores = head_scores(head)
        peak = jnp.max(scores, axis=1, keepdims=True)
        expo = jnp.exp(scores - peak)
        denom = jnp.sum(expo, axis=1, keepdims=True)
        probs = (expo / denom).astype(HALF)
        mixed = lax.dynamic_update_slice_in_dim(
            mixed, product(probs, values), head * head_dim, 1
        )
        logsum = lax.dynamic_update_slice_in_dim(
            logsum, (peak + jnp.log(denom)).reshape(1, total), head, 0
        )
        return (mixed, logsum)

    mixed, logsum = lax.fori_loop(
        0,
        local_heads,
        forward_head,
        (
            jnp.zeros((total, local_heads * head_dim), FULL),
            jnp.zeros((local_heads, total), FULL),
        ),
    )
    attended = (mixed * valid[:, None]).astype(HALF)
    middle = resid + scatter_rows(product(attended, output_copy))
    scale_two = rms_scale(middle)
    rows_two = gather_rows((middle * scale_two * gain_two).astype(HALF))
    gate = product(rows_two, gate_copy)
    upper = product(rows_two, up_copy)
    sigma = jax.nn.sigmoid(gate)
    swish = gate * sigma
    hidden = (swish * upper).astype(HALF)
    layer_out = (middle + scatter_rows(product(hidden, down_copy))).astype(HALF)

    grad_out = cotangent.astype(FULL)
    grad_rows = gather_rows(cotangent)
    down_sum = ring.reduce(
        lambda slot: contract_rows(hidden, grad_rows[:, slot * block : (slot + 1) * block])
    )
    grad_hidden = contract_cols(grad_rows, down_copy)
    grad_gate = (grad_hidden * upper * sigma * (1.0 + gate * (1.0 - sigma))).astype(HALF)
    grad_up = (grad_hidden * swish).astype(HALF)
    gate_sum = ring.reduce(
        lambda slot: contract_rows(rows_two[:, slot * block : (slot + 1) * block], grad_gate)
    )
    up_sum = ring.reduce(
        lambda slot: contract_rows(rows_two[:, slot * block : (slot + 1) * block], grad_up)
    )
    grad_normed_two = scatter_rows(
        contract_cols(grad_gate, gate_copy) + contract_cols(grad_up, up_copy)
    )
    grad_gain_two = jnp.sum(grad_normed_two * middle * scale_two, axis=0)
    inner_two = grad_normed_two * gain_two
    grad_middle = (
        grad_out
        + scale_two * inner_two
        - middle * scale_two**3 * jnp.mean(inner_two * middle, axis=1, keepdims=True)
    )
    middle_rows = gather_rows(grad_middle.astype(HALF))
    output_sum = ring.reduce(
        lambda slot: contract_rows(attended, middle_rows[:, slot * block : (slot + 1) * block])
    )
    grad_mixed = contract_cols(middle_rows, output_copy)
    grad_attended = grad_mixed.astype(HALF) * valid[:, None].astype(HALF)

    def backward_head(head, carry):
        grad_query, grad_key, grad_value = carry
        query_head, scores = head_scores(head)
        lse_row = lax.dynamic_index_in_dim(logsum, head, 0, keepdims=False)
        probs = jnp.exp(scores - lse_row[:, None])
        grad_head = lax.dynamic_slice_in_dim(grad_attended, head * head_dim, head_dim, 1)
        value_term = contract_rows(probs.astype(HALF), grad_head)
        grad_probs = contract_cols(grad_head, values)
        grad_scores = (
            probs * (grad_probs - jnp.sum(probs * grad_probs, axis=1, keepdims=True))
        ).astype(HALF)
        query_term = scale * product(grad_scores, keys)
        key_term = scale * contract_rows(grad_scores, query_head)
        grad_query = lax.dynamic_update_slice_in_dim(grad_query, query_term, head * head_dim, 1)
        grad_key = grad_key + key_term
        grad_value = grad_value + value_term
        return (grad_query, grad_key, grad_value)

    grad_query, grad_key, grad_value = lax.fori_loop(
        0,
        local_heads,
        backward_head,
        (
            jnp.zeros((total, inner), FULL),
            jnp.zeros((total, kv_width), FULL),
            jnp.zeros((total, kv_width), FULL),
        ),
    )
    grad_joined = jnp.concatenate(
        [
            rotate(grad_query, cosine, sine, -1.0).astype(HALF),
            rotate(grad_key, cosine, sine, -1.0).astype(HALF),
            grad_value.astype(HALF),
        ],
        axis=1,
    )
    first_sum = ring.reduce(
        lambda slot: contract_rows(rows_one[:, slot * block : (slot + 1) * block], grad_joined)
    )
    grad_normed_one = scatter_rows(contract_cols(grad_joined, first_copy))
    grad_gain_one = jnp.sum(grad_normed_one * resid * scale_one, axis=0)
    inner_one = grad_normed_one * gain_one
    input_grad = (
        grad_middle
        + scale_one * inner_one
        - resid * scale_one**3 * jnp.mean(inner_one * resid, axis=1, keepdims=True)
    )
    both = jnp.stack([grad_gain_one, grad_gain_two])
    gain_sum = ring.reduce(lambda slot: both[:, slot * block : (slot + 1) * block])
    gain_sum = lax.psum(gain_sum, "tensor")
    return (
        ring.unshuffle(layer_out),
        ring.unshuffle(input_grad),
        first_sum[:, :inner],
        first_sum[:, inner : inner + kv_width],
        first_sum[:, inner + kv_width :],
        output_sum,
        gate_sum,
        up_sum,
        down_sum,
        gain_sum[0],
        gain_sum[1],
    )


def solution(mesh):
    placed = (
        P(("dp", "tensor"), None),
        P("dp", "tensor"),
        P("dp", "tensor"),
        P("dp", "tensor"),
        P("tensor", "dp"),
        P("dp", "tensor"),
        P("dp", "tensor"),
        P("tensor", "dp"),
        P("dp"),
        P("dp"),
        P("dp", None),
        P(("dp", "tensor"), None),
    )
    return jax.shard_map(
        per_device,
        mesh=mesh,
        in_specs=placed,
        out_specs=(
            P(("dp", "tensor"), None),
            P(("dp", "tensor"), None),
            P("dp", "tensor"),
            P("dp", "tensor"),
            P("dp", "tensor"),
            P("tensor", "dp"),
            P("dp", "tensor"),
            P("dp", "tensor"),
            P("tensor", "dp"),
            P("dp"),
            P("dp"),
        ),
        check_vma=False,
    )
```

```python
import functools
import math

import jax
import jax.numpy as jnp
from jax import lax
from jax.experimental import pallas as pl
from jax.experimental.pallas import tpu as pltpu
from jax.sharding import PartitionSpec as P

HEAD_DIM = 64


EPS = 1e-05
NEG = -1e30
HALF = jnp.bfloat16
FULL = jnp.float32


def group_layout(counts, total):
    ends = jnp.cumsum(counts)
    starts = ends - counts
    place = jnp.arange(total, dtype=jnp.int32)
    segment = jnp.sum((place[:, None] >= ends[None, :]).astype(jnp.int32), axis=1)
    bounds = jnp.concatenate([starts, ends[-1:]])
    slots = jnp.arange(bounds.shape[0], dtype=jnp.int32)
    begin = jnp.sum(jnp.where(segment[:, None] == slots[None, :], bounds[None, :], 0), axis=1)
    position = (place - begin).astype(FULL)
    valid = (place < ends[-1]).astype(FULL)
    allowed = (segment[:, None] == segment[None, :]) & (place[None, :] <= place[:, None])
    return (position, valid, allowed)


def angle_tables(position):
    half = HEAD_DIM // 2
    freq = jnp.exp(jnp.arange(half, dtype=FULL) * (-2.0 * math.log(10000.0) / HEAD_DIM))
    angle = position[:, None] * freq[None, :]
    return (jnp.cos(angle), jnp.sin(angle))


def contract_rows(left, right):
    return lax.dot_general(left, right, (((0,), (0,)), ((), ())), preferred_element_type=FULL)


def contract_cols(left, right):
    return lax.dot_general(left, right, (((1,), (1,)), ((), ())), preferred_element_type=FULL)


def product(left, right):
    return jnp.dot(left, right, preferred_element_type=FULL)


def rms_scale(values):
    return lax.rsqrt(jnp.mean(values * values, axis=1, keepdims=True) + EPS)


TILE = 256
VMEM = 56 * 2**20

def lasting(time):
    return pl.CostEstimate(flops=int(time * 1.1e9), bytes_accessed=0, transcendentals=0)


def tie(value, *marks):
    return lax.optimization_barrier((value, marks))[0]


def nt(left, right):
    return lax.dot_general(left, right, (((1,), (1,)), ((), ())), preferred_element_type=FULL)

def nn(left, right):
    return lax.dot_general(left, right, (((1,), (0,)), ((), ())), preferred_element_type=FULL)

def swap_halves(x):
    lane = lax.broadcasted_iota(jnp.int32, x.shape, 1)
    return jnp.where(lane % 64 < 32, pltpu.roll(x, 96, 1), pltpu.roll(x, 32, 1))

def fill_bias(begin_ref, bias_ref, total):
    for i in range(total // TILE):
        size = (i + 1) * TILE
        key = lax.broadcasted_iota(jnp.int32, (size, TILE), 0)
        query = lax.broadcasted_iota(jnp.int32, (size, TILE), 1) + i * TILE
        begin = begin_ref[:, i * TILE:(i + 1) * TILE]
        keep = (key >= begin) & (key <= query)
        bias_ref[i, 0:size, :] = jnp.where(keep, 0.0, NEG)

def fwd_kernel(joined_ref, cos_ref, sin_ref, begin_ref, valid_ref, q_ref, kv_ref, out_ref, lse_ref, bias_ref, ka_ref, vt_ref):
    total, wide = joined_ref.shape
    pairs = wide // 128 - 1
    lane = lax.broadcasted_iota(jnp.int32, (total, 128), 1)
    kv = joined_ref[:, pairs * 128:]
    cosine = cos_ref[...]
    sine = sin_ref[...]
    turned = kv * cosine + swap_halves(kv) * sine
    kv = jnp.where(lane < 64, turned, kv)
    kv_ref[...] = kv.astype(HALF)
    ka_ref[0] = jnp.where(lane < 64, kv, 0.0).astype(HALF)
    ka_ref[1] = jnp.where(lane < 64, 0.0, pltpu.roll(kv, 64, 1)).astype(HALF)
    vt_ref[...] = kv.T[64:, :].astype(HALF)
    fill_bias(begin_ref, bias_ref, total)
    for p in range(pairs):
        q = joined_ref[:, p * 128:(p + 1) * 128]
        q_ref[:, p * 128:(p + 1) * 128] = ((q * cosine + swap_halves(q) * sine) * (HEAD_DIM ** -0.5)).astype(HALF)

    def pair(p, carry):
        column = pl.multiple_of(p * 128, 128)
        for i in range(total // TILE):
            size = (i + 1) * TILE
            q = q_ref[i * TILE:(i + 1) * TILE, pl.ds(column, 128)]
            parts = []
            for a in range(2):
                s = nt(ka_ref[a, 0:size, :], q) + bias_ref[i, 0:size, :]
                peak = jnp.max(s, axis=0, keepdims=True)
                expo = jnp.exp(s - peak)
                denom = jnp.sum(expo, axis=0, keepdims=True)
                o = nn(vt_ref[:, 0:size], expo.astype(HALF)) / denom
                lse_ref[2 * p + a, :, i * TILE:(i + 1) * TILE] = peak + jnp.log(denom)
                parts.append(o)
            o = jnp.concatenate(parts, axis=0) * valid_ref[:, i * TILE:(i + 1) * TILE]
            out_ref[i * TILE:(i + 1) * TILE, pl.ds(column, 128)] = o.T.astype(HALF)
        return carry
    lax.fori_loop(0, pairs, pair, 0)

def attend(joined, cosine, sine, begin, valid):
    total, wide = joined.shape
    heads = wide // 64 - 2
    return pl.pallas_call(
        fwd_kernel,
        out_shape=(
            jax.ShapeDtypeStruct((total, heads * 64), HALF),
            jax.ShapeDtypeStruct((total, 128), HALF),
            jax.ShapeDtypeStruct((total, heads * 64), HALF),
            jax.ShapeDtypeStruct((heads, 1, total), FULL),
        ),
        scratch_shapes=[
            pltpu.VMEM((total // TILE, total, TILE), FULL),
            pltpu.VMEM((2, total, 128), HALF),
            pltpu.VMEM((64, total), HALF),
        ],
        compiler_params=pltpu.CompilerParams(vmem_limit_bytes=VMEM),
        cost_estimate=lasting(13.0),
        name="attend",
    )(joined, cosine, sine, begin, valid)

def bwd_kernel(q_ref, kv_ref, do_ref, lse_ref, cos_ref, sin_ref, begin_ref, out_ref, bias_ref, ka_ref, va_ref, kt_ref, dk_ref, dv_ref):
    total = kv_ref.shape[0]
    pairs = q_ref.shape[1] // 128
    lane = lax.broadcasted_iota(jnp.int32, (total, 128), 1)
    kv = kv_ref[...].astype(FULL)
    rolled = pltpu.roll(kv, 64, 1)
    ka_ref[0] = jnp.where(lane < 64, kv, 0.0).astype(HALF)
    ka_ref[1] = jnp.where(lane < 64, 0.0, rolled).astype(HALF)
    va_ref[0] = jnp.where(lane < 64, rolled, 0.0).astype(HALF)
    va_ref[1] = jnp.where(lane < 64, 0.0, kv).astype(HALF)
    kt_ref[...] = kv.T[:64, :].astype(HALF)
    dk_ref[...] = jnp.zeros_like(dk_ref)
    dv_ref[...] = jnp.zeros_like(dv_ref)
    fill_bias(begin_ref, bias_ref, total)
    low = lax.broadcasted_iota(jnp.int32, (TILE, 128), 1) < 64

    def pair(p, carry):
        column = pl.multiple_of(p * 128, 128)
        for i in range(total // TILE):
            size = (i + 1) * TILE
            rows = slice(i * TILE, (i + 1) * TILE)
            q = q_ref[rows, pl.ds(column, 128)]
            do = do_ref[rows, pl.ds(column, 128)]
            parts = []
            for a in range(2):
                keep = low if a == 0 else jnp.logical_not(low)
                s = nt(ka_ref[a, 0:size, :], q) + bias_ref[i, 0:size, :]
                probs = jnp.exp(s - lse_ref[2 * p + a, :, rows])
                dprobs = nt(va_ref[a, 0:size, :], do)
                delta = jnp.sum(probs * dprobs, axis=0, keepdims=True)
                ds = (probs * (dprobs - delta)).astype(HALF)
                dv_ref[0:size, :] += nn(probs.astype(HALF), jnp.where(keep, do, jnp.zeros_like(do)))
                dk_ref[0:size, :] += nn(ds, jnp.where(keep, q, jnp.zeros_like(q)))
                parts.append(nn(kt_ref[:, 0:size], ds))
            dq = jnp.concatenate(parts, axis=0).T * (HEAD_DIM ** -0.5)
            dq = dq * cos_ref[rows, :] - swap_halves(dq) * sin_ref[rows, :]
            out_ref[rows, pl.ds(column, 128)] = dq.astype(HALF)
        return carry
    lax.fori_loop(0, pairs, pair, 0)
    dk = dk_ref[...]
    dk = dk + pltpu.roll(dk, 64, 1)
    dk = dk * cos_ref[...] - swap_halves(dk) * sin_ref[...]
    dv = dv_ref[...]
    dv = dv + pltpu.roll(dv, 64, 1)
    out_ref[:, pairs * 128:] = jnp.where(lane < 64, dk, dv).astype(HALF)

def attend_back(q, kv, do, lse, cosine, sine, begin):
    total, wide = q.shape
    return pl.pallas_call(
        bwd_kernel,
        out_shape=jax.ShapeDtypeStruct((total, wide + 128), HALF),
        scratch_shapes=[
            pltpu.VMEM((total // TILE, total, TILE), FULL),
            pltpu.VMEM((2, total, 128), HALF),
            pltpu.VMEM((2, total, 128), HALF),
            pltpu.VMEM((64, total), HALF),
            pltpu.VMEM((total, 128), FULL),
            pltpu.VMEM((total, 128), FULL),
        ],
        compiler_params=pltpu.CompilerParams(vmem_limit_bytes=VMEM),
        cost_estimate=lasting(14.5),
        name="attend_back",
    )(q, kv, do, lse, cosine, sine, begin)


def block_of(refs, slot, extent, slots):
    if slot < slots - 1 or len(refs) == slots:
        return refs[slot][0:extent, :]
    cut = refs[-2].shape[0]
    return jnp.concatenate([refs[-2][...], refs[-1][0 : extent - cut, :]], axis=0)


def whole(array):
    return pl.BlockSpec(array.shape, lambda i: (0,) * array.ndim)

def rows_of(width, tile=TILE):
    return pl.BlockSpec((tile, width), lambda i: (i, 0))

def gate_up_kernel(units, x_ref, grad_ref, *refs):
    pieces, hidden_ref, out_ref = refs[:-2], refs[-2], refs[-1]
    for start in range(0, units, 128):
        there = slice(start, start + 128)
        pairs = [
            jnp.concatenate([ref[:, there], ref[:, units + start : units + start + 128]], axis=1)
            for ref in pieces
        ]
        both = nn(x_ref[...], jnp.concatenate(pairs, axis=0))
        gate, up = both[:, :128], both[:, 128:]
        sigma = jax.nn.sigmoid(gate)
        swish = gate * sigma
        grad = grad_ref[:, there]
        hidden_ref[:, there] = (swish * up).astype(HALF)
        out_ref[:, there] = (grad * up * sigma * (1.0 + gate * (1.0 - sigma))).astype(HALF)
        out_ref[:, units + start : units + start + 128] = (grad * swish).astype(HALF)


def gate_up(x, grad, pieces):
    total, wide = x.shape
    units = pieces[0].shape[1] // 2
    return pl.pallas_call(
        functools.partial(gate_up_kernel, units),
        grid=(total // TILE,),
        in_specs=[rows_of(wide), rows_of(units)] + [whole(p) for p in pieces],
        out_specs=[rows_of(units), rows_of(2 * units)],
        out_shape=(
            jax.ShapeDtypeStruct((total, units), HALF),
            jax.ShapeDtypeStruct((total, 2 * units), HALF),
        ),
        compiler_params=pltpu.CompilerParams(vmem_limit_bytes=VMEM),
        cost_estimate=lasting(16.5),
        name="gate_up",
    )(x, grad, *pieces)


def hidden_back_kernel(slots, x_ref, *refs):
    pieces, out_ref = refs[:-1], refs[-1]
    units, depth = pieces[0].shape
    total = None
    for slot in range(slots):
        part = nt(x_ref[:, slot * depth : (slot + 1) * depth], block_of(pieces, slot, units, slots))
        total = part if total is None else total + part
    out_ref[...] = total


def hidden_back(x, pieces, slots):
    total, wide = x.shape
    units = pieces[0].shape[0]
    return pl.pallas_call(
        functools.partial(hidden_back_kernel, slots),
        grid=(total // TILE,),
        in_specs=[rows_of(wide)] + [whole(p) for p in pieces],
        out_specs=rows_of(units),
        out_shape=jax.ShapeDtypeStruct((total, units), FULL),
        compiler_params=pltpu.CompilerParams(vmem_limit_bytes=VMEM),
        cost_estimate=lasting(10.8),
        name="hidden_back",
    )(x, *pieces)


def outward_kernel(slots, depth, view, transposed, x_ref, *refs):
    pieces, out_ref = refs[:-1], refs[-1]
    for slot in range(slots):
        block = view(block_of(pieces, slot, depth, slots))
        part = nt(x_ref[...], block) if transposed else nn(x_ref[...], block)
        width = part.shape[1]
        out_ref[:, slot * width : (slot + 1) * width] = part.astype(HALF)


def outward(x, pieces, slots, depth, width, transposed, time, name, view=lambda block: block):
    total, wide = x.shape
    return pl.pallas_call(
        functools.partial(outward_kernel, slots, depth, view, transposed),
        grid=(total // TILE,),
        in_specs=[rows_of(wide)] + [whole(p) for p in pieces],
        out_specs=rows_of(slots * width),
        out_shape=jax.ShapeDtypeStruct((total, slots * width), HALF),
        compiler_params=pltpu.CompilerParams(vmem_limit_bytes=VMEM),
        cost_estimate=lasting(time),
        name=name,
    )(x, *pieces)


def output_view(depth, start, block):
    packed = block[:depth, start:]
    return jnp.concatenate(
        [packed[:, at : at + depth] for at in range(0, packed.shape[1], depth)], axis=0
    )


def first_kernel(slots, depth, x_ref, *refs):
    pieces = refs[:-3]
    normed_ref, joined_ref, gains_ref = refs[-3:]
    values = x_ref[...].astype(FULL)
    values = values * lax.rsqrt(jnp.mean(values * values, axis=1, keepdims=True) + EPS)
    parts = []
    for slot in range(slots):
        there = slice(slot * depth, (slot + 1) * depth)
        block = block_of(pieces, slot, pieces[0].shape[0], slots)
        gains = block[depth:, :depth].astype(FULL)[0:2]
        gains_ref[:, there] = gains
        normed_ref[:, there] = (values[:, there] * gains[0:1]).astype(HALF)
        parts.append(block[:depth, : joined_ref.shape[1]])
    joined_ref[...] = nn(normed_ref[...], jnp.concatenate(parts, axis=0))


def first(x, pieces, slots, depth, units):
    total, wide = x.shape
    return pl.pallas_call(
        functools.partial(first_kernel, slots, depth),
        grid=(total // TILE,),
        in_specs=[rows_of(wide)] + [whole(p) for p in pieces],
        out_specs=[rows_of(wide), rows_of(units), pl.BlockSpec((2, wide), lambda i: (0, 0))],
        out_shape=(
            jax.ShapeDtypeStruct((total, wide), HALF),
            jax.ShapeDtypeStruct((total, units), FULL),
            jax.ShapeDtypeStruct((2, wide), FULL),
        ),
        compiler_params=pltpu.CompilerParams(vmem_limit_bytes=VMEM),
        cost_estimate=lasting(7.0),
        name="first",
    )(x, *pieces)


def first_back_kernel(slots, depth, grad_ref, x_ref, *refs):
    pieces = refs[:-2]
    out_ref, gain_ref = refs[-2:]

    @pl.when(pl.program_id(0) == 0)
    def _():
        gain_ref[...] = jnp.zeros_like(gain_ref)

    values = x_ref[...].astype(FULL)
    values = values * lax.rsqrt(jnp.mean(values * values, axis=1, keepdims=True) + EPS)
    for slot in range(slots):
        there = slice(slot * depth, (slot + 1) * depth)
        block = block_of(pieces, slot, pieces[0].shape[0], slots)[:depth, : grad_ref.shape[1]]
        part = nt(grad_ref[...], block).astype(HALF)
        out_ref[:, there] = part
        gain_ref[:, there] += jnp.sum(part.astype(FULL) * values[:, there], axis=0, keepdims=True)


def first_back(grad, x, pieces, slots, depth):
    total, wide = x.shape
    return pl.pallas_call(
        functools.partial(first_back_kernel, slots, depth),
        grid=(total // TILE,),
        in_specs=[rows_of(grad.shape[1]), rows_of(wide)] + [whole(p) for p in pieces],
        out_specs=[rows_of(wide), pl.BlockSpec((1, wide), lambda i: (0, 0))],
        out_shape=(jax.ShapeDtypeStruct((total, wide), HALF), jax.ShapeDtypeStruct((1, wide), FULL)),
        compiler_params=pltpu.CompilerParams(vmem_limit_bytes=VMEM),
        cost_estimate=lasting(7.0),
        name="first_back",
    )(grad, x, *pieces)


def mixed_back_kernel(slots, view, x_ref, *refs):
    pieces, valid_ref, out_ref = refs[:-2], refs[-2], refs[-1]
    total = None
    for slot in range(slots):
        block = view(block_of(pieces, slot, pieces[0].shape[0], slots))
        width = block.shape[1]
        part = nt(x_ref[:, slot * width : (slot + 1) * width], block)
        total = part if total is None else total + part
    out_ref[...] = (total.astype(HALF).astype(FULL) * valid_ref[...]).astype(HALF)


def mixed_back(x, pieces, valid, slots, units, view):
    total, wide = x.shape
    return pl.pallas_call(
        functools.partial(mixed_back_kernel, slots, view),
        grid=(total // TILE,),
        in_specs=[rows_of(wide)] + [whole(p) for p in pieces] + [rows_of(1)],
        out_specs=rows_of(units),
        out_shape=jax.ShapeDtypeStruct((total, units), HALF),
        compiler_params=pltpu.CompilerParams(vmem_limit_bytes=VMEM),
        cost_estimate=lasting(5.4),
        name="mixed_back",
    )(x, *pieces, valid)


def shuffle_kernel(members, count, inverse, *refs):
    half = len(refs) // 2
    for source, target in zip(refs[:half], refs[half:]):
        width = source.shape[1] // count
        for slot, member in enumerate(members()):
            there = pl.ds(pl.multiple_of(member * width, width), width)
            here = slice(slot * width, (slot + 1) * width)
            if inverse:
                target[:, there] = source[:, here]
            else:
                target[:, here] = source[:, there]


def join_kernel(*refs):
    out_ref = refs[-1]
    mine = lax.axis_index("tensor")
    count = refs[0].shape[0]
    for index, ref in enumerate(refs[:-1]):
        out_ref[pl.ds(pl.multiple_of((mine ^ index) * count, count), count), :] = ref[...]


def ring_order(count):
    return list(range(0, count, 2)) + list(range(count - 1, 0, -2))


class Ring:
    def __init__(self, count):
        self.count = count
        self.half = count // 2
        order = ring_order(count)
        self.up = [(order[i], order[(i + 1) % count]) for i in range(count)]
        self.down = [(b, a) for a, b in self.up]
        self.offsets = [0]
        for step in range(1, self.half):
            self.offsets += [-step, step]
        self.offsets.append(self.half)

    def members(self):
        count = self.count
        index = lax.axis_index("dp")
        here = jnp.where(index % 2 == 0, index // 2, count - 1 - index // 2)
        spots = [lax.rem(here + (offset + count), count) for offset in self.offsets]
        return [jnp.where(spot < count // 2, 2 * spot, 2 * (count - 1 - spot) + 1) for spot in spots]

    def shuffle(self, *arrays, inverse=False):
        if arrays[0].shape[1] // self.count % 128:
            return [self.shuffle_narrow(array, inverse) for array in arrays]
        return pl.pallas_call(
            functools.partial(shuffle_kernel, self.members, self.count, inverse),
            out_shape=[jax.ShapeDtypeStruct(array.shape, array.dtype) for array in arrays],
            compiler_params=pltpu.CompilerParams(vmem_limit_bytes=VMEM),
            cost_estimate=lasting(1.5),
            name="shuffle",
        )(*arrays)

    def shuffle_narrow(self, values, inverse):
        width = values.shape[1] // self.count
        if not inverse:
            pieces = [lax.dynamic_slice_in_dim(values, m * width, width, 1) for m in self.members()]
            return jnp.concatenate(pieces, axis=1)
        out = jnp.zeros_like(values)
        for slot, member in enumerate(self.members()):
            piece = values[:, slot * width : (slot + 1) * width]
            out = lax.dynamic_update_slice_in_dim(out, piece, member * width, 1)
        return out

    def gather(self, shard):
        pieces = [shard]
        marks = []
        above = below = shard
        for _ in range(1, self.half):
            above = lax.ppermute(above, "dp", self.up)
            below = lax.ppermute(below, "dp", self.down)
            pieces += [above, below]
            marks.append((above, below))
        cut = shard.shape[0] // 2
        upper = lax.ppermute(above[:cut], "dp", self.up)
        lower = lax.ppermute(below[cut:], "dp", self.down)
        pieces += [upper, lower]
        marks.append((upper, lower))
        return pieces, marks

    def reduce_far(self, far):
        cut = far.shape[0] // 2
        above = lax.ppermute(far[:cut].astype(HALF), "dp", self.up)
        below = lax.ppermute(far[cut:].astype(HALF), "dp", self.down)
        return above, below

    def reduce_second(self, part, first):
        above, below = first
        cut = above.shape[0]
        top = part(self.count - 2).astype(FULL)
        low = part(self.count - 3).astype(FULL)
        top = jnp.concatenate([top[:cut] + above.astype(FULL), top[cut:]], axis=0)
        low = jnp.concatenate([low[:cut], low[cut:] + below.astype(FULL)], axis=0)
        return top.astype(HALF), low.astype(HALF)

    def reduce(self, part, second=None):
        if second is None:
            second = self.reduce_second(part, self.reduce_far(part(self.count - 1)))
        top, low = second
        arrived, sent = [], []
        for step in range(self.half - 1, 0, -1):
            if step < self.half - 1:
                top = (part(2 * step).astype(FULL) + above.astype(FULL)).astype(HALF)
                low = (part(2 * step - 1).astype(FULL) + below.astype(FULL)).astype(HALF)
            above = lax.ppermute(top, "dp", self.up)
            below = lax.ppermute(low, "dp", self.down)
            sent.append((top, low))
            arrived.append((above, below))
        return part(0).astype(FULL) + above.astype(FULL) + below.astype(FULL), arrived, sent

    def gather_rows(self, rows):
        first = lax.ppermute(rows, "tensor", beside(2))
        near = lax.ppermute(rows, "tensor", beside(1))
        far = lax.ppermute(first, "tensor", beside(1))
        return pl.pallas_call(
            join_kernel,
            out_shape=jax.ShapeDtypeStruct((4 * rows.shape[0], rows.shape[1]), rows.dtype),
            compiler_params=pltpu.CompilerParams(vmem_limit_bytes=VMEM),
            cost_estimate=lasting(2.0),
            name="join",
        )(rows, near, first, far)

    def scatter_rows(self, values):
        mine = lax.axis_index("tensor")
        count = values.shape[0] // 4

        def piece(index):
            return lax.dynamic_slice_in_dim(values, (mine ^ index) * count, count, 0)

        across = lax.ppermute(piece(3), "tensor", beside(1)).astype(FULL)
        near = lax.ppermute(piece(1), "tensor", beside(1)).astype(FULL)
        send = (piece(2).astype(FULL) + across).astype(HALF)
        far = lax.ppermute(send, "tensor", beside(2)).astype(FULL)
        return piece(0).astype(FULL) + near + far

    def lengths(self, counts):
        return counts[0]


def beside(index):
    return [(i, i ^ index) for i in range(4)]


def per_device(
    tokens,
    query_weight,
    key_weight,
    value_weight,
    output_weight,
    gate_weight,
    up_weight,
    down_weight,
    attention_gain,
    feed_gain,
    doc_lengths,
    cotangent,
):
    ring = Ring(lax.axis_size("dp"))
    own_rows, width = tokens.shape
    block = query_weight.shape[0]

    inner = query_weight.shape[1]
    kv_width = key_weight.shape[1]
    joint = inner + 2 * kv_width
    units = gate_weight.shape[1]
    slots = ring.count
    output_shard = output_weight.astype(HALF)
    gains = jnp.stack([attention_gain, feed_gain]).astype(HALF)
    first_shard = jnp.concatenate(
        [
            jnp.concatenate([query_weight, key_weight, value_weight], axis=1).astype(HALF),
            *[output_shard[at : at + block] for at in range(0, inner, block)],
        ],
        axis=1,
    )
    gains = jnp.pad(gains, ((0, 30), (0, first_shard.shape[1] - block)))
    first_shard = jnp.concatenate([first_shard, gains], axis=0)
    first_pieces, first_marks = ring.gather(first_shard)
    down_pieces, down_marks = ring.gather(tie(down_weight.astype(HALF), first_marks[-2]))
    feed_shard = jnp.concatenate([gate_weight, up_weight], axis=1).astype(HALF)
    feed_pieces, feed_marks = ring.gather(tie(feed_shard, down_marks[-2]))
    tokens, cotangent = ring.shuffle(tie(tokens, first_shard), cotangent)
    view = functools.partial(output_view, block, joint)

    total = own_rows * lax.axis_size("tensor")
    position, valid, allowed = group_layout(ring.lengths(doc_lengths), total)
    begin = (jnp.arange(total, dtype=jnp.int32) - position.astype(jnp.int32)).reshape(1, total)
    cosine, sine = angle_tables(position)
    cosine = jnp.tile(cosine, (1, 4))
    sine = jnp.concatenate([-sine, sine, -sine, sine], axis=1)
    resid = tokens.astype(FULL)
    scale_one = rms_scale(resid)
    rows_in = ring.gather_rows(tokens)
    rows_one, joined, gains = first(rows_in, first_pieces, slots, block, joint)
    gain_one, gain_two = gains[0], gains[1]
    queries, keys_values, attended, logsum = attend(
        tie(joined, down_marks[0]), cosine, sine, begin, valid.reshape(1, total)
    )
    middle = resid + ring.scatter_rows(
        outward(
            tie(attended, down_marks[1]),
            first_pieces,
            slots,
            first_shard.shape[0],
            block,
            False,
            5.2,
            "output",
            view,
        )
    )
    scale_two = rms_scale(middle)
    rows_two = ring.gather_rows((middle * scale_two * gain_two).astype(HALF))
    grad_out = cotangent.astype(FULL)
    grad_rows = ring.gather_rows(cotangent)
    grad_hidden = hidden_back(grad_rows, down_pieces, slots)
    hidden, grad_feed = gate_up(rows_two, grad_hidden, feed_pieces)

    mid, far = (slots - 3) * block, (slots - 1) * block
    feed_far = contract_rows(rows_two[:, far:], grad_feed).astype(HALF)
    down_far = contract_rows(hidden, grad_rows[:, far:]).astype(HALF)
    feed_first = ring.reduce_far(feed_far)
    down_first = ring.reduce_far(down_far)
    partial_two = outward(
        tie(grad_feed, feed_far, down_far), feed_pieces, slots, block, block, True, 16.2, "feed_back"
    )
    rows_mid, hidden_mid = tie((rows_two, hidden), partial_two, feed_first, down_first)
    feed_mid = contract_rows(rows_mid[:, mid:far], grad_feed).astype(HALF)
    down_mid = contract_rows(hidden_mid, grad_rows[:, mid:far]).astype(HALF)
    feed_near = down_near = None

    def feed_part(slot):
        if slot >= slots - 3:
            return feed_mid[(slot - slots + 3) * block :][:block]
        return feed_near[slot * block : (slot + 1) * block]

    def down_part(slot):
        if slot >= slots - 3:
            return down_mid[:, (slot - slots + 3) * block :][:, :block]
        return down_near[:, slot * block : (slot + 1) * block]

    feed_second = ring.reduce_second(feed_part, feed_first)
    down_second = ring.reduce_second(down_part, down_first)
    rows_near, hidden_near = tie((rows_two, hidden), feed_second, down_second)
    feed_near = contract_rows(rows_near[:, :mid], grad_feed).astype(HALF)
    down_near = contract_rows(hidden_near, grad_rows[:, :mid]).astype(HALF)
    feed_sum, feed_steps, feed_sent = ring.reduce(feed_part, feed_second)
    down_sum, down_steps, down_sent = ring.reduce(down_part, down_second)
    grad_normed_two = ring.scatter_rows(partial_two)
    grad_gain_two = jnp.sum(grad_normed_two * middle * scale_two, axis=0)
    inner_two = grad_normed_two * gain_two
    grad_middle = (
        grad_out
        + scale_two * inner_two
        - middle * scale_two**3 * jnp.mean(inner_two * middle, axis=1, keepdims=True)
    )
    middle_rows = ring.gather_rows(grad_middle.astype(HALF))
    grad_attended = mixed_back(tie(middle_rows, feed_sent[1], down_sent[1]), first_pieces, valid[:, None], slots, inner, view)
    grad_joined = attend_back(queries, keys_values, grad_attended, logsum, cosine, sine, begin)
    late_joined = tie(grad_joined, feed_sent[2], down_sent[2])
    first_sum, _, _ = ring.reduce(
        lambda slot: contract_rows(rows_one[:, slot * block : (slot + 1) * block], late_joined)
    )
    partial_one, grad_gain_one = first_back(late_joined, rows_in, first_pieces, slots, block)
    both = jnp.concatenate([grad_gain_one, grad_gain_two[None]], axis=0)

    def output_part(slot):
        there = slice(slot * block, (slot + 1) * block)
        extra = jnp.pad(both[:, there], ((0, 30), (0, 0)))
        return jnp.concatenate([contract_rows(attended, middle_rows[:, there]), extra], axis=0)

    output_sum, _, _ = ring.reduce(output_part)
    gain_sum = lax.psum(output_sum[inner : inner + 2], "tensor")
    output_sum = output_sum[:inner]
    layer_out = (
        middle
        + ring.scatter_rows(
            outward(tie(hidden, grad_joined), down_pieces, slots, units, block, False, 9.2, "down")
        )
    ).astype(HALF)
    grad_normed_one = ring.scatter_rows(partial_one)
    inner_one = grad_normed_one * gain_one
    input_grad = (
        grad_middle
        + scale_one * inner_one
        - resid * scale_one**3 * jnp.mean(inner_one * resid, axis=1, keepdims=True)
    )
    layer_out, input_grad = ring.shuffle(layer_out, input_grad, inverse=True)
    return (
        layer_out,
        input_grad,
        first_sum[:, :inner],
        first_sum[:, inner : inner + kv_width],
        first_sum[:, inner + kv_width :],
        output_sum,
        feed_sum[:, :units],
        feed_sum[:, units:],
        down_sum,
        gain_sum[0],
        gain_sum[1],
    )


def solution(mesh):
    placed = (
        P(("dp", "tensor"), None),
        P("dp", "tensor"),
        P("dp", "tensor"),
        P("dp", "tensor"),
        P("tensor", "dp"),
        P("dp", "tensor"),
        P("dp", "tensor"),
        P("tensor", "dp"),
        P("dp"),
        P("dp"),
        P("dp", None),
        P(("dp", "tensor"), None),
    )
    return jax.shard_map(
        per_device,
        mesh=mesh,
        in_specs=placed,
        out_specs=(
            P(("dp", "tensor"), None),
            P(("dp", "tensor"), None),
            P("dp", "tensor"),
            P("dp", "tensor"),
            P("dp", "tensor"),
            P("tensor", "dp"),
            P("dp", "tensor"),
            P("dp", "tensor"),
            P("tensor", "dp"),
            P("dp"),
            P("dp"),
        ),
        check_vma=False,
    )
```

```python
import functools
import math

import jax
import jax.numpy as jnp
from jax import lax
from jax.experimental import pallas as pl
from jax.experimental.pallas import tpu as pltpu
from jax.sharding import PartitionSpec as P

HEAD_DIM = 64


EPS = 1e-05
NEG = -1e30
HALF = jnp.bfloat16
FULL = jnp.float32


def group_layout(counts, total):
    ends = jnp.cumsum(counts)
    starts = ends - counts
    place = jnp.arange(total, dtype=jnp.int32)
    segment = jnp.sum((place[:, None] >= ends[None, :]).astype(jnp.int32), axis=1)
    bounds = jnp.concatenate([starts, ends[-1:]])
    slots = jnp.arange(bounds.shape[0], dtype=jnp.int32)
    begin = jnp.sum(jnp.where(segment[:, None] == slots[None, :], bounds[None, :], 0), axis=1)
    position = (place - begin).astype(FULL)
    valid = (place < ends[-1]).astype(FULL)
    allowed = (segment[:, None] == segment[None, :]) & (place[None, :] <= place[:, None])
    return (position, valid, allowed)


def angle_tables(position):
    half = HEAD_DIM // 2
    freq = jnp.exp(jnp.arange(half, dtype=FULL) * (-2.0 * math.log(10000.0) / HEAD_DIM))
    angle = position[:, None] * freq[None, :]
    return (jnp.cos(angle), jnp.sin(angle))


def contract_rows(left, right):
    return lax.dot_general(left, right, (((0,), (0,)), ((), ())), preferred_element_type=FULL)


def contract_cols(left, right):
    return lax.dot_general(left, right, (((1,), (1,)), ((), ())), preferred_element_type=FULL)


def product(left, right):
    return jnp.dot(left, right, preferred_element_type=FULL)


def rms_scale(values):
    return lax.rsqrt(jnp.mean(values * values, axis=1, keepdims=True) + EPS)


TILE = 256
VMEM = 56 * 2**20

def lasting(time):
    return pl.CostEstimate(flops=int(time * 1.1e9), bytes_accessed=0, transcendentals=0)


def tie(value, *marks):
    return lax.optimization_barrier((value, marks))[0]


def nt(left, right):
    return lax.dot_general(left, right, (((1,), (1,)), ((), ())), preferred_element_type=FULL)

def nn(left, right):
    return lax.dot_general(left, right, (((1,), (0,)), ((), ())), preferred_element_type=FULL)

def swap_halves(x):
    lane = lax.broadcasted_iota(jnp.int32, x.shape, 1)
    return jnp.where(lane % 64 < 32, pltpu.roll(x, 96, 1), pltpu.roll(x, 32, 1))

def fill_bias(begin_ref, bias_ref, total):
    for i in range(total // TILE):
        size = (i + 1) * TILE
        key = lax.broadcasted_iota(jnp.int32, (size, TILE), 0)
        query = lax.broadcasted_iota(jnp.int32, (size, TILE), 1) + i * TILE
        begin = begin_ref[:, i * TILE:(i + 1) * TILE]
        keep = (key >= begin) & (key <= query)
        bias_ref[i, 0:size, :] = jnp.where(keep, 0.0, NEG)

def fwd_kernel(joined_ref, cos_ref, sin_ref, begin_ref, valid_ref, q_ref, kv_ref, out_ref, lse_ref, bias_ref, ka_ref, vt_ref):
    total, wide = joined_ref.shape
    pairs = wide // 128 - 1
    lane = lax.broadcasted_iota(jnp.int32, (total, 128), 1)
    kv = joined_ref[:, pairs * 128:]
    cosine = cos_ref[...]
    sine = sin_ref[...]
    turned = kv * cosine + swap_halves(kv) * sine
    kv = jnp.where(lane < 64, turned, kv)
    kv_ref[...] = kv.astype(HALF)
    ka_ref[0] = jnp.where(lane < 64, kv, 0.0).astype(HALF)
    ka_ref[1] = jnp.where(lane < 64, 0.0, pltpu.roll(kv, 64, 1)).astype(HALF)
    vt_ref[...] = kv.T[64:, :].astype(HALF)
    fill_bias(begin_ref, bias_ref, total)
    for p in range(pairs):
        q = joined_ref[:, p * 128:(p + 1) * 128]
        q_ref[:, p * 128:(p + 1) * 128] = ((q * cosine + swap_halves(q) * sine) * (HEAD_DIM ** -0.5)).astype(HALF)

    def pair(p, carry):
        column = pl.multiple_of(p * 128, 128)
        for i in range(total // TILE):
            size = (i + 1) * TILE
            q = q_ref[i * TILE:(i + 1) * TILE, pl.ds(column, 128)]
            parts = []
            for a in range(2):
                s = nt(ka_ref[a, 0:size, :], q) + bias_ref[i, 0:size, :]
                peak = jnp.max(s, axis=0, keepdims=True)
                expo = jnp.exp(s - peak)
                denom = jnp.sum(expo, axis=0, keepdims=True)
                o = nn(vt_ref[:, 0:size], expo.astype(HALF)) / denom
                lse_ref[2 * p + a, :, i * TILE:(i + 1) * TILE] = peak + jnp.log(denom)
                parts.append(o)
            o = jnp.concatenate(parts, axis=0) * valid_ref[:, i * TILE:(i + 1) * TILE]
            out_ref[i * TILE:(i + 1) * TILE, pl.ds(column, 128)] = o.T.astype(HALF)
        return carry
    lax.fori_loop(0, pairs, pair, 0)

def attend(joined, cosine, sine, begin, valid):
    total, wide = joined.shape
    heads = wide // 64 - 2
    return pl.pallas_call(
        fwd_kernel,
        out_shape=(
            jax.ShapeDtypeStruct((total, heads * 64), HALF),
            jax.ShapeDtypeStruct((total, 128), HALF),
            jax.ShapeDtypeStruct((total, heads * 64), HALF),
            jax.ShapeDtypeStruct((heads, 1, total), FULL),
        ),
        scratch_shapes=[
            pltpu.VMEM((total // TILE, total, TILE), FULL),
            pltpu.VMEM((2, total, 128), HALF),
            pltpu.VMEM((64, total), HALF),
        ],
        compiler_params=pltpu.CompilerParams(vmem_limit_bytes=VMEM),
        cost_estimate=lasting(13.0),
        name="attend",
    )(joined, cosine, sine, begin, valid)

def bwd_kernel(q_ref, kv_ref, do_ref, lse_ref, cos_ref, sin_ref, begin_ref, out_ref, bias_ref, ka_ref, va_ref, kt_ref, dk_ref, dv_ref):
    total = kv_ref.shape[0]
    pairs = q_ref.shape[1] // 128
    lane = lax.broadcasted_iota(jnp.int32, (total, 128), 1)
    kv = kv_ref[...].astype(FULL)
    rolled = pltpu.roll(kv, 64, 1)
    ka_ref[0] = jnp.where(lane < 64, kv, 0.0).astype(HALF)
    ka_ref[1] = jnp.where(lane < 64, 0.0, rolled).astype(HALF)
    va_ref[0] = jnp.where(lane < 64, rolled, 0.0).astype(HALF)
    va_ref[1] = jnp.where(lane < 64, 0.0, kv).astype(HALF)
    kt_ref[...] = kv.T[:64, :].astype(HALF)
    dk_ref[...] = jnp.zeros_like(dk_ref)
    dv_ref[...] = jnp.zeros_like(dv_ref)
    fill_bias(begin_ref, bias_ref, total)
    low = lax.broadcasted_iota(jnp.int32, (TILE, 128), 1) < 64

    def pair(p, carry):
        column = pl.multiple_of(p * 128, 128)
        for i in range(total // TILE):
            size = (i + 1) * TILE
            rows = slice(i * TILE, (i + 1) * TILE)
            q = q_ref[rows, pl.ds(column, 128)]
            do = do_ref[rows, pl.ds(column, 128)]
            parts = []
            for a in range(2):
                keep = low if a == 0 else jnp.logical_not(low)
                s = nt(ka_ref[a, 0:size, :], q) + bias_ref[i, 0:size, :]
                probs = jnp.exp(s - lse_ref[2 * p + a, :, rows])
                dprobs = nt(va_ref[a, 0:size, :], do)
                delta = jnp.sum(probs * dprobs, axis=0, keepdims=True)
                ds = (probs * (dprobs - delta)).astype(HALF)
                dv_ref[0:size, :] += nn(probs.astype(HALF), jnp.where(keep, do, jnp.zeros_like(do)))
                dk_ref[0:size, :] += nn(ds, jnp.where(keep, q, jnp.zeros_like(q)))
                parts.append(nn(kt_ref[:, 0:size], ds))
            dq = jnp.concatenate(parts, axis=0).T * (HEAD_DIM ** -0.5)
            dq = dq * cos_ref[rows, :] - swap_halves(dq) * sin_ref[rows, :]
            out_ref[rows, pl.ds(column, 128)] = dq.astype(HALF)
        return carry
    lax.fori_loop(0, pairs, pair, 0)
    dk = dk_ref[...]
    dk = dk + pltpu.roll(dk, 64, 1)
    dk = dk * cos_ref[...] - swap_halves(dk) * sin_ref[...]
    dv = dv_ref[...]
    dv = dv + pltpu.roll(dv, 64, 1)
    out_ref[:, pairs * 128:] = jnp.where(lane < 64, dk, dv).astype(HALF)

def attend_back(q, kv, do, lse, cosine, sine, begin):
    total, wide = q.shape
    return pl.pallas_call(
        bwd_kernel,
        out_shape=jax.ShapeDtypeStruct((total, wide + 128), HALF),
        scratch_shapes=[
            pltpu.VMEM((total // TILE, total, TILE), FULL),
            pltpu.VMEM((2, total, 128), HALF),
            pltpu.VMEM((2, total, 128), HALF),
            pltpu.VMEM((64, total), HALF),
            pltpu.VMEM((total, 128), FULL),
            pltpu.VMEM((total, 128), FULL),
        ],
        compiler_params=pltpu.CompilerParams(vmem_limit_bytes=VMEM),
        cost_estimate=lasting(0.0),
        name="attend_back",
    )(q, kv, do, lse, cosine, sine, begin)


def block_of(refs, slot, extent, slots):
    if slot < slots - 1 or len(refs) == slots:
        return refs[slot][0:extent, :]
    cut = refs[-2].shape[0]
    return jnp.concatenate([refs[-2][...], refs[-1][0 : extent - cut, :]], axis=0)


def whole(array):
    return pl.BlockSpec(array.shape, lambda i: (0,) * array.ndim)

def rows_of(width, tile=TILE):
    return pl.BlockSpec((tile, width), lambda i: (i, 0))

def gate_up_kernel(units, x_ref, grad_ref, *refs):
    pieces, hidden_ref, out_ref = refs[:-2], refs[-2], refs[-1]
    for start in range(0, units, 128):
        there = slice(start, start + 128)
        pairs = [
            jnp.concatenate([ref[:, there], ref[:, units + start : units + start + 128]], axis=1)
            for ref in pieces
        ]
        both = nn(x_ref[...], jnp.concatenate(pairs, axis=0))
        gate, up = both[:, :128], both[:, 128:]
        sigma = jax.nn.sigmoid(gate)
        swish = gate * sigma
        grad = grad_ref[:, there]
        hidden_ref[:, there] = (swish * up).astype(HALF)
        out_ref[:, there] = (grad * up * sigma * (1.0 + gate * (1.0 - sigma))).astype(HALF)
        out_ref[:, units + start : units + start + 128] = (grad * swish).astype(HALF)


def gate_up(x, grad, pieces):
    total, wide = x.shape
    units = pieces[0].shape[1] // 2
    return pl.pallas_call(
        functools.partial(gate_up_kernel, units),
        grid=(total // TILE,),
        in_specs=[rows_of(wide), rows_of(units)] + [whole(p) for p in pieces],
        out_specs=[rows_of(units), rows_of(2 * units)],
        out_shape=(
            jax.ShapeDtypeStruct((total, units), HALF),
            jax.ShapeDtypeStruct((total, 2 * units), HALF),
        ),
        compiler_params=pltpu.CompilerParams(vmem_limit_bytes=VMEM),
        cost_estimate=lasting(16.5),
        name="gate_up",
    )(x, grad, *pieces)


def hidden_back_kernel(slots, x_ref, *refs):
    pieces, out_ref = refs[:-1], refs[-1]
    units, depth = pieces[0].shape
    total = None
    for slot in range(slots):
        part = nt(x_ref[:, slot * depth : (slot + 1) * depth], block_of(pieces, slot, units, slots))
        total = part if total is None else total + part
    out_ref[...] = total


def hidden_back(x, pieces, slots):
    total, wide = x.shape
    units = pieces[0].shape[0]
    return pl.pallas_call(
        functools.partial(hidden_back_kernel, slots),
        grid=(total // TILE,),
        in_specs=[rows_of(wide)] + [whole(p) for p in pieces],
        out_specs=rows_of(units),
        out_shape=jax.ShapeDtypeStruct((total, units), FULL),
        compiler_params=pltpu.CompilerParams(vmem_limit_bytes=VMEM),
        cost_estimate=lasting(10.8),
        name="hidden_back",
    )(x, *pieces)


def feed_grads_kernel(early, x_ref, feed_ref, grad_ref, hidden_ref, *out_refs):
    wide = feed_ref.shape[1]
    half = x_ref.shape[1] // 2
    over_rows = (((0,), (0,)), ((), ()))

    def make(write):
        for left, right, there in (
            (x_ref, feed_ref, slice(0, wide)),
            (grad_ref, hidden_ref, slice(wide, wide + hidden_ref.shape[1])),
        ):
            part = lax.dot_general(left[...], right[...], over_rows, preferred_element_type=FULL)
            write(there, part.astype(HALF))

    def write_whole(there, part):
        out_refs[-1][:, there] = part

    def write_halves(there, part):
        out_refs[0][:, there] = part[:half]
        out_refs[1][:, there] = part[half:]

    if early:
        pl.when(pl.program_id(0) == 0)(functools.partial(make, write_halves))
        pl.when(pl.program_id(0) > 0)(functools.partial(make, write_whole))
    else:
        make(write_whole)


def feed_grads(x, feed, grad, hidden, slots, block, early):
    total = x.shape[0]
    units = hidden.shape[1]
    if block % 128:
        parts = []
        for start, stop in ((slots - 1, slots), (slots - 3, slots - 1)) if early else ((0, slots - 3),):
            there = slice(start * block, stop * block)
            part = [contract_rows(x[:, there], feed), contract_rows(grad[:, there], hidden)]
            parts.append(jnp.concatenate(part, axis=1).astype(HALF))
        return [*jnp.split(parts[0], 2), parts[1]] if early else parts
    place = (lambda i: (0, slots - 1 - i)) if early else (lambda i: (0, i))
    columns = pl.BlockSpec((total, block), place)
    shapes = [(block // 2, 3 * units)] * 2 + [(2 * block, 3 * units)] if early else [((slots - 3) * block, 3 * units)]
    out_specs = [pl.BlockSpec((block, 3 * units), (lambda i: (2 - jnp.maximum(i, 1), 0)) if early else (lambda i: (i, 0)))]
    if early:
        out_specs = [pl.BlockSpec((block // 2, 3 * units), lambda i: (0, 0))] * 2 + out_specs
    return pl.pallas_call(
        functools.partial(feed_grads_kernel, early),
        grid=(3 if early else slots - 3,),
        in_specs=[columns, whole(feed), columns, whole(hidden)],
        out_specs=out_specs,
        out_shape=[jax.ShapeDtypeStruct(shape, HALF) for shape in shapes],
        compiler_params=pltpu.CompilerParams(vmem_limit_bytes=VMEM),
        cost_estimate=lasting(0.0),
        name="feed_grads",
    )(x, feed, grad, hidden)


def outward_kernel(slots, depth, view, transposed, x_ref, *refs):
    pieces, out_ref = refs[:-1], refs[-1]
    for slot in range(slots):
        block = view(block_of(pieces, slot, depth, slots))
        part = nt(x_ref[...], block) if transposed else nn(x_ref[...], block)
        width = part.shape[1]
        out_ref[:, slot * width : (slot + 1) * width] = part.astype(HALF)


def outward(x, pieces, slots, depth, width, transposed, time, name, view=lambda block: block):
    total, wide = x.shape
    return pl.pallas_call(
        functools.partial(outward_kernel, slots, depth, view, transposed),
        grid=(total // TILE,),
        in_specs=[rows_of(wide)] + [whole(p) for p in pieces],
        out_specs=rows_of(slots * width),
        out_shape=jax.ShapeDtypeStruct((total, slots * width), HALF),
        compiler_params=pltpu.CompilerParams(vmem_limit_bytes=VMEM),
        cost_estimate=lasting(time),
        name=name,
    )(x, *pieces)


def output_view(depth, start, block):
    packed = block[:depth, start:]
    return jnp.concatenate(
        [packed[:, at : at + depth] for at in range(0, packed.shape[1], depth)], axis=0
    )


def first_kernel(slots, depth, x_ref, *refs):
    pieces = refs[:-3]
    normed_ref, joined_ref, gains_ref = refs[-3:]
    values = x_ref[...].astype(FULL)
    values = values * lax.rsqrt(jnp.mean(values * values, axis=1, keepdims=True) + EPS)
    parts = []
    for slot in range(slots):
        there = slice(slot * depth, (slot + 1) * depth)
        block = block_of(pieces, slot, pieces[0].shape[0], slots)
        gains = block[depth:, :depth].astype(FULL)[0:2]
        gains_ref[:, there] = gains
        normed_ref[:, there] = (values[:, there] * gains[0:1]).astype(HALF)
        parts.append(block[:depth, : joined_ref.shape[1]])
    joined_ref[...] = nn(normed_ref[...], jnp.concatenate(parts, axis=0))


def first(x, pieces, slots, depth, units):
    total, wide = x.shape
    return pl.pallas_call(
        functools.partial(first_kernel, slots, depth),
        grid=(total // TILE,),
        in_specs=[rows_of(wide)] + [whole(p) for p in pieces],
        out_specs=[rows_of(wide), rows_of(units), pl.BlockSpec((2, wide), lambda i: (0, 0))],
        out_shape=(
            jax.ShapeDtypeStruct((total, wide), HALF),
            jax.ShapeDtypeStruct((total, units), FULL),
            jax.ShapeDtypeStruct((2, wide), FULL),
        ),
        compiler_params=pltpu.CompilerParams(vmem_limit_bytes=VMEM),
        cost_estimate=lasting(7.0),
        name="first",
    )(x, *pieces)


def first_back_kernel(slots, depth, grad_ref, *refs):
    pieces, out_ref = refs[:-1], refs[-1]
    for slot in range(slots):
        block = block_of(pieces, slot, pieces[0].shape[0], slots)[:depth, : grad_ref.shape[1]]
        out_ref[:, slot * depth : (slot + 1) * depth] = nt(grad_ref[...], block).astype(HALF)


def first_back(grad, pieces, slots, depth):
    total, wide = grad.shape
    return pl.pallas_call(
        functools.partial(first_back_kernel, slots, depth),
        grid=(total // TILE,),
        in_specs=[rows_of(wide)] + [whole(p) for p in pieces],
        out_specs=rows_of(slots * depth),
        out_shape=jax.ShapeDtypeStruct((total, slots * depth), HALF),
        compiler_params=pltpu.CompilerParams(vmem_limit_bytes=VMEM),
        cost_estimate=lasting(0.0),
        name="first_back",
    )(grad, *pieces)


def mixed_back_kernel(slots, view, x_ref, *refs):
    pieces, valid_ref, out_ref = refs[:-2], refs[-2], refs[-1]
    total = None
    for slot in range(slots):
        block = view(block_of(pieces, slot, pieces[0].shape[0], slots))
        width = block.shape[1]
        part = nt(x_ref[:, slot * width : (slot + 1) * width], block)
        total = part if total is None else total + part
    out_ref[...] = (total.astype(HALF).astype(FULL) * valid_ref[...]).astype(HALF)


def mixed_back(x, pieces, valid, slots, units, view):
    total, wide = x.shape
    return pl.pallas_call(
        functools.partial(mixed_back_kernel, slots, view),
        grid=(total // TILE,),
        in_specs=[rows_of(wide)] + [whole(p) for p in pieces] + [rows_of(1)],
        out_specs=rows_of(units),
        out_shape=jax.ShapeDtypeStruct((total, units), HALF),
        compiler_params=pltpu.CompilerParams(vmem_limit_bytes=VMEM),
        cost_estimate=lasting(0.0),
        name="mixed_back",
    )(x, *pieces, valid)


def shuffle_kernel(members, count, inverse, *refs):
    half = len(refs) // 2
    for source, target in zip(refs[:half], refs[half:]):
        width = source.shape[1] // count
        for slot, member in enumerate(members()):
            there = pl.ds(pl.multiple_of(member * width, width), width)
            here = slice(slot * width, (slot + 1) * width)
            if inverse:
                target[:, there] = source[:, here]
            else:
                target[:, here] = source[:, there]


def join_kernel(*refs):
    out_ref = refs[-1]
    mine = lax.axis_index("tensor")
    count = refs[0].shape[0]
    for index, ref in enumerate(refs[:-1]):
        out_ref[pl.ds(pl.multiple_of((mine ^ index) * count, count), count), :] = ref[...]


class Travel:
    def __init__(self, ring, shard):
        self.ring = ring
        self.pieces = [shard]
        self.marks = []
        self.above = self.below = shard

    def step(self, *after):
        ring = self.ring
        if after:
            self.above, self.below = tie((self.above, self.below), *after)
        if len(self.marks) == ring.half - 1:
            cut = self.above.shape[0] // 2
            self.above, self.below = self.above[:cut], self.below[cut:]
        self.above = lax.ppermute(self.above, "dp", ring.up)
        self.below = lax.ppermute(self.below, "dp", ring.down)
        self.pieces += [self.above, self.below]
        self.marks.append((self.above, self.below))

    def steps(self, count):
        for _ in range(count):
            self.step()
        return self


class Homeward:
    def __init__(self, ring, part, far):
        self.ring = ring
        self.part = part
        self.left = ring.half - 1
        self.cut = far[0].shape[0]
        self.send(*far)

    def send(self, top, low):
        self.above = lax.ppermute(top, "dp", self.ring.up)
        self.below = lax.ppermute(low, "dp", self.ring.down)
        self.sent, self.arrived = (top, low), (self.above, self.below)

    def total(self, slot, arrived, upper):
        own = self.part(slot)
        first = 0 if upper else own.shape[0] - arrived.shape[0]
        last = first + arrived.shape[0]
        joined = (own[first:last].astype(FULL) + arrived.astype(FULL)).astype(HALF)
        return jnp.concatenate([own[:first], joined, own[last:]], axis=0)

    def step(self, *after):
        above, below = self.above, self.below
        if after:
            above, below = tie((above, below), *after)
        top = self.total(2 * self.left, above, True)
        low = self.total(2 * self.left - 1, below, False)
        self.left -= 1
        self.send(top, low)
        return self

    def steps(self, count):
        for _ in range(count):
            self.step()
        return self

    def own(self):
        return self.part(0).astype(FULL) + self.above.astype(FULL) + self.below.astype(FULL)


def ring_order(count):
    return list(range(0, count, 2)) + list(range(count - 1, 0, -2))


class Ring:
    def __init__(self, count):
        self.count = count
        self.half = count // 2
        order = ring_order(count)
        self.up = [(order[i], order[(i + 1) % count]) for i in range(count)]
        self.down = [(b, a) for a, b in self.up]
        self.offsets = [0]
        for step in range(1, self.half):
            self.offsets += [-step, step]
        self.offsets.append(self.half)

    def members(self):
        count = self.count
        index = lax.axis_index("dp")
        here = jnp.where(index % 2 == 0, index // 2, count - 1 - index // 2)
        spots = [lax.rem(here + (offset + count), count) for offset in self.offsets]
        return [jnp.where(spot < count // 2, 2 * spot, 2 * (count - 1 - spot) + 1) for spot in spots]

    def shuffle(self, *arrays, inverse=False):
        if arrays[0].shape[1] // self.count % 128:
            return [self.shuffle_narrow(array, inverse) for array in arrays]
        return pl.pallas_call(
            functools.partial(shuffle_kernel, self.members, self.count, inverse),
            out_shape=[jax.ShapeDtypeStruct(array.shape, array.dtype) for array in arrays],
            compiler_params=pltpu.CompilerParams(vmem_limit_bytes=VMEM),
            cost_estimate=lasting(1.5),
            name="shuffle",
        )(*arrays)

    def shuffle_narrow(self, values, inverse):
        width = values.shape[1] // self.count
        if not inverse:
            pieces = [lax.dynamic_slice_in_dim(values, m * width, width, 1) for m in self.members()]
            return jnp.concatenate(pieces, axis=1)
        out = jnp.zeros_like(values)
        for slot, member in enumerate(self.members()):
            piece = values[:, slot * width : (slot + 1) * width]
            out = lax.dynamic_update_slice_in_dim(out, piece, member * width, 1)
        return out

    def gather(self, shard):
        return Travel(self, shard)

    def gather_rows(self, rows):
        first = lax.ppermute(rows, "tensor", beside(2))
        near = lax.ppermute(rows, "tensor", beside(1))
        far = lax.ppermute(first, "tensor", beside(1))
        return pl.pallas_call(
            join_kernel,
            out_shape=jax.ShapeDtypeStruct((4 * rows.shape[0], rows.shape[1]), rows.dtype),
            compiler_params=pltpu.CompilerParams(vmem_limit_bytes=VMEM),
            cost_estimate=lasting(2.0),
            name="join",
        )(rows, near, first, far)

    def scatter_rows(self, values):
        mine = lax.axis_index("tensor")
        count = values.shape[0] // 4

        def piece(index):
            return lax.dynamic_slice_in_dim(values, (mine ^ index) * count, count, 0)

        given = jnp.concatenate([piece(3), piece(1)], axis=0)
        given = lax.ppermute(given, "tensor", beside(1)).astype(FULL)
        send = (piece(2).astype(FULL) + given[:count]).astype(HALF)
        far = lax.ppermute(send, "tensor", beside(2)).astype(FULL)
        return piece(0).astype(FULL) + given[count:] + far

    def lengths(self, counts):
        return counts[0]


def beside(index):
    return [(i, i ^ index) for i in range(4)]


def per_device(
    tokens,
    query_weight,
    key_weight,
    value_weight,
    output_weight,
    gate_weight,
    up_weight,
    down_weight,
    attention_gain,
    feed_gain,
    doc_lengths,
    cotangent,
):
    ring = Ring(lax.axis_size("dp"))
    own_rows, width = tokens.shape
    block = query_weight.shape[0]

    inner = query_weight.shape[1]
    kv_width = key_weight.shape[1]
    joint = inner + 2 * kv_width
    units = gate_weight.shape[1]
    slots = ring.count
    output_shard = output_weight.astype(HALF)
    gains = jnp.stack([attention_gain, feed_gain]).astype(HALF)
    first_shard = jnp.concatenate(
        [
            jnp.concatenate([query_weight, key_weight, value_weight], axis=1).astype(HALF),
            *[output_shard[at : at + block] for at in range(0, inner, block)],
        ],
        axis=1,
    )
    gains = jnp.pad(gains, ((0, 30), (0, first_shard.shape[1] - block)))
    first_shard = jnp.concatenate([first_shard, gains], axis=0)
    whole_way = ring.half
    first_travel = ring.gather(first_shard).steps(whole_way)
    first_pieces, first_marks = first_travel.pieces, first_travel.marks
    down_travel = ring.gather(tie(down_weight.astype(HALF), first_marks[-2])).steps(whole_way)
    down_pieces, down_marks = down_travel.pieces, down_travel.marks
    feed_shard = jnp.concatenate([gate_weight, up_weight], axis=1).astype(HALF)
    feed_pieces = ring.gather(tie(feed_shard, down_marks[-2])).steps(whole_way).pieces
    tokens, cotangent = ring.shuffle(tie(tokens, first_shard), cotangent)
    view = functools.partial(output_view, block, joint)

    total = own_rows * lax.axis_size("tensor")
    position, valid, allowed = group_layout(ring.lengths(doc_lengths), total)
    begin = (jnp.arange(total, dtype=jnp.int32) - position.astype(jnp.int32)).reshape(1, total)
    cosine, sine = angle_tables(position)
    cosine = jnp.tile(cosine, (1, 4))
    sine = jnp.concatenate([-sine, sine, -sine, sine], axis=1)
    resid = tokens.astype(FULL)
    scale_one = rms_scale(resid)
    rows_in = ring.gather_rows(tokens)
    grad_rows = ring.gather_rows(cotangent)
    rows_one, joined, gains = first(
        tie(rows_in, down_marks[0]), first_pieces, slots, block, joint
    )
    gain_one, gain_two = gains[0], gains[1]
    queries, keys_values, attended, logsum = attend(
        tie(joined, down_marks[1]), cosine, sine, begin, valid.reshape(1, total)
    )
    middle = resid + ring.scatter_rows(
        outward(
            tie(attended, down_marks[2]),
            first_pieces,
            slots,
            first_shard.shape[0],
            block,
            False,
            5.2,
            "output",
            view,
        )
    )
    scale_two = rms_scale(middle)
    rows_two = ring.gather_rows((middle * scale_two * gain_two).astype(HALF))
    grad_out = cotangent.astype(FULL)
    grad_hidden = hidden_back(grad_rows, down_pieces, slots)
    hidden, grad_feed = gate_up(rows_two, grad_hidden, feed_pieces)

    *feed_far, feed_mid = feed_grads(rows_two, grad_feed, grad_rows, hidden, slots, block, True)
    feed_near = None

    def feed_part(slot):
        if slot >= slots - 3:
            return feed_mid[(slot - slots + 3) * block :][:block]
        return feed_near[slot * block : (slot + 1) * block]

    feed_sums = Homeward(ring, feed_part, feed_far)
    partial_two = outward(
        tie(grad_feed, feed_mid), feed_pieces, slots, block, block, True, 0.0, "feed_back"
    )
    feed_sums.step(partial_two)
    grad_normed_two = ring.scatter_rows(partial_two)
    inner_two = grad_normed_two * gain_two
    grad_middle = (
        grad_out
        + scale_two * inner_two
        - middle * scale_two**3 * jnp.mean(inner_two * middle, axis=1, keepdims=True)
    )
    middle_given = grad_middle.astype(HALF)
    middle_rows = ring.gather_rows(middle_given)
    (feed_near,) = feed_grads(
        tie(rows_two, feed_sums.sent, middle_given), grad_feed, grad_rows, hidden, slots, block, False
    )
    partial_out = outward(
        tie(hidden, feed_near), down_pieces, slots, units, block, False, 0.0, "down"
    )
    feed_sums.step(partial_out).steps(ring.half - 4)
    grad_attended = mixed_back(
        tie(middle_rows, feed_sums.sent), first_pieces, valid[:, None], slots, inner, view
    )
    grad_joined = attend_back(queries, keys_values, grad_attended, logsum, cosine, sine, begin)
    last_grad = jnp.concatenate(
        [
            contract_rows(rows_one, grad_joined).astype(HALF),
            contract_rows(middle_rows, attended).astype(HALF),
        ],
        axis=1,
    )
    partial_one = first_back(tie(grad_joined, last_grad), first_pieces, slots, block)

    def last_part(slot):
        return last_grad[slot * block : (slot + 1) * block]

    last_sums = Homeward(ring, last_part, jnp.split(last_part(slots - 1), 2))
    last_sums.step(partial_one)
    feed_sums.step(last_sums.sent)
    last_sums.step(feed_sums.sent).steps(ring.half - 4).step(feed_sums.arrived)
    feed_sum, last_sum = feed_sums.own(), last_sums.own()
    first_sum = last_sum[:, :joint]
    output_sum = last_sum[:, joint:].T
    layer_out = (
        middle
        + ring.scatter_rows(partial_out)
    ).astype(HALF)
    grad_normed_one = ring.scatter_rows(partial_one)
    inner_one = grad_normed_one * gain_one
    input_grad = (
        grad_middle
        + scale_one * inner_one
        - resid * scale_one**3 * jnp.mean(inner_one * resid, axis=1, keepdims=True)
    )
    layer_out, input_grad = ring.shuffle(layer_out, input_grad, inverse=True)
    gain_sums = [
        jnp.sum(grads * shard.astype(FULL), axis=1) / gain.astype(HALF).astype(FULL)
        for grads, shard, gain in (
            (first_sum, first_shard[:block, :joint], attention_gain),
            (feed_sum[:, : 2 * units], feed_shard, feed_gain),
        )
    ]
    gain_sums = lax.psum(jnp.stack(gain_sums), "tensor")
    return (
        layer_out,
        input_grad,
        first_sum[:, :inner],
        first_sum[:, inner : inner + kv_width],
        first_sum[:, inner + kv_width :],
        output_sum,
        feed_sum[:, :units],
        feed_sum[:, units : 2 * units],
        feed_sum[:, 2 * units :].T,
        gain_sums[0],
        gain_sums[1],
    )


def solution(mesh):
    placed = (
        P(("dp", "tensor"), None),
        P("dp", "tensor"),
        P("dp", "tensor"),
        P("dp", "tensor"),
        P("tensor", "dp"),
        P("dp", "tensor"),
        P("dp", "tensor"),
        P("tensor", "dp"),
        P("dp"),
        P("dp"),
        P("dp", None),
        P(("dp", "tensor"), None),
    )
    return jax.shard_map(
        per_device,
        mesh=mesh,
        in_specs=placed,
        out_specs=(
            P(("dp", "tensor"), None),
            P(("dp", "tensor"), None),
            P("dp", "tensor"),
            P("dp", "tensor"),
            P("dp", "tensor"),
            P("tensor", "dp"),
            P("dp", "tensor"),
            P("dp", "tensor"),
            P("tensor", "dp"),
            P("dp"),
            P("dp"),
        ),
        check_vma=False,
    )
```

```python
import functools
import math

import jax
import jax.numpy as jnp
from jax import lax
from jax.experimental import pallas as pl
from jax.experimental.pallas import tpu as pltpu
from jax.sharding import PartitionSpec as P

HEAD_DIM = 64


EPS = 1e-05
NEG = -1e30
HALF = jnp.bfloat16
FULL = jnp.float32


def group_layout(counts, total):
    ends = jnp.cumsum(counts)
    starts = ends - counts
    place = jnp.arange(total, dtype=jnp.int32)
    segment = jnp.sum((place[:, None] >= ends[None, :]).astype(jnp.int32), axis=1)
    bounds = jnp.concatenate([starts, ends[-1:]])
    slots = jnp.arange(bounds.shape[0], dtype=jnp.int32)
    begin = jnp.sum(jnp.where(segment[:, None] == slots[None, :], bounds[None, :], 0), axis=1)
    position = (place - begin).astype(FULL)
    valid = (place < ends[-1]).astype(FULL)
    allowed = (segment[:, None] == segment[None, :]) & (place[None, :] <= place[:, None])
    return (position, valid, allowed)


def angle_tables(position):
    half = HEAD_DIM // 2
    freq = jnp.exp(jnp.arange(half, dtype=FULL) * (-2.0 * math.log(10000.0) / HEAD_DIM))
    angle = position[:, None] * freq[None, :]
    return (jnp.cos(angle), jnp.sin(angle))


def contract_rows(left, right):
    return lax.dot_general(left, right, (((0,), (0,)), ((), ())), preferred_element_type=FULL)


def contract_cols(left, right):
    return lax.dot_general(left, right, (((1,), (1,)), ((), ())), preferred_element_type=FULL)


def product(left, right):
    return jnp.dot(left, right, preferred_element_type=FULL)


def rms_scale(values):
    return lax.rsqrt(jnp.mean(values * values, axis=1, keepdims=True) + EPS)


TILE = 256
VMEM = 24 * 2**20

def lasting(time):
    return pl.CostEstimate(flops=int(time * 1.1e9), bytes_accessed=0, transcendentals=0)


def tie(value, *marks):
    return lax.optimization_barrier((value, marks))[0]


def nt(left, right):
    return lax.dot_general(left, right, (((1,), (1,)), ((), ())), preferred_element_type=FULL)

def nn(left, right):
    return lax.dot_general(left, right, (((1,), (0,)), ((), ())), preferred_element_type=FULL)

def swap_halves(x):
    lane = lax.broadcasted_iota(jnp.int32, x.shape, 1)
    return jnp.where(lane % 64 < 32, pltpu.roll(x, 96, 1), pltpu.roll(x, 32, 1))

def fill_bias(begin_ref, bias_ref, total):
    for i in range(total // TILE):
        size = (i + 1) * TILE
        key = lax.broadcasted_iota(jnp.int32, (size, TILE), 0)
        query = lax.broadcasted_iota(jnp.int32, (size, TILE), 1) + i * TILE
        begin = begin_ref[:, i * TILE:(i + 1) * TILE]
        keep = (key >= begin) & (key <= query)
        bias_ref[i, 0:size, :] = jnp.where(keep, 0.0, NEG)

def fwd_kernel(joined_ref, cos_ref, sin_ref, begin_ref, valid_ref, q_ref, kv_ref, out_ref, lse_ref, bias_ref, ka_ref, vt_ref):
    total, wide = joined_ref.shape
    pairs = wide // 128 - 1
    lane = lax.broadcasted_iota(jnp.int32, (total, 128), 1)
    kv = joined_ref[:, pairs * 128:]
    cosine = cos_ref[...]
    sine = sin_ref[...]
    turned = kv * cosine + swap_halves(kv) * sine
    kv = jnp.where(lane < 64, turned, kv)
    kv_ref[...] = kv.astype(HALF)
    ka_ref[0] = jnp.where(lane < 64, kv, 0.0).astype(HALF)
    ka_ref[1] = jnp.where(lane < 64, 0.0, pltpu.roll(kv, 64, 1)).astype(HALF)
    vt_ref[...] = kv.T[64:, :].astype(HALF)
    fill_bias(begin_ref, bias_ref, total)
    for p in range(pairs):
        q = joined_ref[:, p * 128:(p + 1) * 128]
        q_ref[:, p * 128:(p + 1) * 128] = ((q * cosine + swap_halves(q) * sine) * (HEAD_DIM ** -0.5)).astype(HALF)

    def pair(p, carry):
        column = pl.multiple_of(p * 128, 128)
        for i in range(total // TILE):
            size = (i + 1) * TILE
            q = q_ref[i * TILE:(i + 1) * TILE, pl.ds(column, 128)]
            parts = []
            for a in range(2):
                s = nt(ka_ref[a, 0:size, :], q) + bias_ref[i, 0:size, :]
                peak = jnp.max(s, axis=0, keepdims=True)
                expo = jnp.exp(s - peak)
                denom = jnp.sum(expo, axis=0, keepdims=True)
                o = nn(vt_ref[:, 0:size], expo.astype(HALF)) / denom
                lse_ref[2 * p + a, :, i * TILE:(i + 1) * TILE] = peak + jnp.log(denom)
                parts.append(o)
            o = jnp.concatenate(parts, axis=0) * valid_ref[:, i * TILE:(i + 1) * TILE]
            out_ref[i * TILE:(i + 1) * TILE, pl.ds(column, 128)] = o.T.astype(HALF)
        return carry
    lax.fori_loop(0, pairs, pair, 0)

def attend(joined, cosine, sine, begin, valid):
    total, wide = joined.shape
    heads = wide // 64 - 2
    return pl.pallas_call(
        fwd_kernel,
        out_shape=(
            jax.ShapeDtypeStruct((total, heads * 64), HALF),
            jax.ShapeDtypeStruct((total, 128), HALF),
            jax.ShapeDtypeStruct((total, heads * 64), HALF),
            jax.ShapeDtypeStruct((heads, 1, total), FULL),
        ),
        scratch_shapes=[
            pltpu.VMEM((total // TILE, total, TILE), FULL),
            pltpu.VMEM((2, total, 128), HALF),
            pltpu.VMEM((64, total), HALF),
        ],
        compiler_params=pltpu.CompilerParams(vmem_limit_bytes=VMEM),
        cost_estimate=lasting(0.0),
        name="attend",
    )(joined, cosine, sine, begin, valid)

def bwd_kernel(q_ref, kv_ref, do_ref, lse_ref, cos_ref, sin_ref, begin_ref, out_ref, bias_ref, ka_ref, va_ref, kt_ref, dk_ref, dv_ref):
    total = kv_ref.shape[0]
    pairs = q_ref.shape[1] // 128
    lane = lax.broadcasted_iota(jnp.int32, (total, 128), 1)
    kv = kv_ref[...].astype(FULL)
    rolled = pltpu.roll(kv, 64, 1)
    ka_ref[0] = jnp.where(lane < 64, kv, 0.0).astype(HALF)
    ka_ref[1] = jnp.where(lane < 64, 0.0, rolled).astype(HALF)
    va_ref[0] = jnp.where(lane < 64, rolled, 0.0).astype(HALF)
    va_ref[1] = jnp.where(lane < 64, 0.0, kv).astype(HALF)
    kt_ref[...] = kv.T[:64, :].astype(HALF)
    dk_ref[...] = jnp.zeros_like(dk_ref)
    dv_ref[...] = jnp.zeros_like(dv_ref)
    fill_bias(begin_ref, bias_ref, total)
    low = lax.broadcasted_iota(jnp.int32, (TILE, 128), 1) < 64

    def pair(p, carry):
        column = pl.multiple_of(p * 128, 128)
        for i in range(total // TILE):
            size = (i + 1) * TILE
            rows = slice(i * TILE, (i + 1) * TILE)
            q = q_ref[rows, pl.ds(column, 128)]
            do = do_ref[rows, pl.ds(column, 128)]
            parts = []
            for a in range(2):
                keep = low if a == 0 else jnp.logical_not(low)
                s = nt(ka_ref[a, 0:size, :], q) + bias_ref[i, 0:size, :]
                probs = jnp.exp(s - lse_ref[2 * p + a, :, rows])
                dprobs = nt(va_ref[a, 0:size, :], do)
                delta = jnp.sum(probs * dprobs, axis=0, keepdims=True)
                ds = (probs * (dprobs - delta)).astype(HALF)
                dv_ref[0:size, :] += nn(probs.astype(HALF), jnp.where(keep, do, jnp.zeros_like(do)))
                dk_ref[0:size, :] += nn(ds, jnp.where(keep, q, jnp.zeros_like(q)))
                parts.append(nn(kt_ref[:, 0:size], ds))
            dq = jnp.concatenate(parts, axis=0).T * (HEAD_DIM ** -0.5)
            dq = dq * cos_ref[rows, :] - swap_halves(dq) * sin_ref[rows, :]
            out_ref[rows, pl.ds(column, 128)] = dq.astype(HALF)
        return carry
    lax.fori_loop(0, pairs, pair, 0)
    dk = dk_ref[...]
    dk = dk + pltpu.roll(dk, 64, 1)
    dk = dk * cos_ref[...] - swap_halves(dk) * sin_ref[...]
    dv = dv_ref[...]
    dv = dv + pltpu.roll(dv, 64, 1)
    out_ref[:, pairs * 128:] = jnp.where(lane < 64, dk, dv).astype(HALF)

def attend_back(q, kv, do, lse, cosine, sine, begin):
    total, wide = q.shape
    return pl.pallas_call(
        bwd_kernel,
        out_shape=jax.ShapeDtypeStruct((total, wide + 128), HALF),
        scratch_shapes=[
            pltpu.VMEM((total // TILE, total, TILE), FULL),
            pltpu.VMEM((2, total, 128), HALF),
            pltpu.VMEM((2, total, 128), HALF),
            pltpu.VMEM((64, total), HALF),
            pltpu.VMEM((total, 128), FULL),
            pltpu.VMEM((total, 128), FULL),
        ],
        compiler_params=pltpu.CompilerParams(vmem_limit_bytes=VMEM),
        cost_estimate=lasting(0.0),
        name="attend_back",
    )(q, kv, do, lse, cosine, sine, begin)


def block_of(refs, slot, extent, slots):
    if slot < slots - 1 or len(refs) == slots:
        return refs[slot][0:extent, :]
    cut = refs[-2].shape[0]
    return jnp.concatenate([refs[-2][...], refs[-1][0 : extent - cut, :]], axis=0)


def whole(array):
    return pl.BlockSpec(memory_space=pltpu.VMEM)

def rows_of(width, tile=TILE):
    return pl.BlockSpec((tile, width), lambda i: (i, 0))

def gate_up_kernel(units, x_ref, grad_ref, *refs):
    pieces, hidden_ref, out_ref = refs[:-2], refs[-2], refs[-1]
    for start in range(0, units, 128):
        there = slice(start, start + 128)
        pairs = [
            jnp.concatenate([ref[:, there], ref[:, units + start : units + start + 128]], axis=1)
            for ref in pieces
        ]
        both = nn(x_ref[...], jnp.concatenate(pairs, axis=0))
        gate, up = both[:, :128], both[:, 128:]
        sigma = jax.nn.sigmoid(gate)
        swish = gate * sigma
        grad = grad_ref[:, there]
        hidden_ref[:, there] = (swish * up).astype(HALF)
        out_ref[:, there] = (grad * up * sigma * (1.0 + gate * (1.0 - sigma))).astype(HALF)
        out_ref[:, units + start : units + start + 128] = (grad * swish).astype(HALF)


def gate_up(x, grad, pieces):
    total, wide = x.shape
    units = pieces[0].shape[1] // 2
    return pl.pallas_call(
        functools.partial(gate_up_kernel, units),
        grid=(total // TILE,),
        in_specs=[rows_of(wide), rows_of(units)] + [whole(p) for p in pieces],
        out_specs=[rows_of(units), rows_of(2 * units)],
        out_shape=(
            jax.ShapeDtypeStruct((total, units), HALF),
            jax.ShapeDtypeStruct((total, 2 * units), HALF),
        ),
        compiler_params=pltpu.CompilerParams(vmem_limit_bytes=VMEM),
        cost_estimate=lasting(16.5),
        name="gate_up",
    )(x, grad, *pieces)


def hidden_back_kernel(slots, x_ref, *refs):
    pieces, out_ref = refs[:-1], refs[-1]
    units, depth = pieces[0].shape
    total = None
    for slot in range(slots):
        part = nt(x_ref[:, slot * depth : (slot + 1) * depth], block_of(pieces, slot, units, slots))
        total = part if total is None else total + part
    out_ref[...] = total


def hidden_back(x, pieces, slots):
    total, wide = x.shape
    units = pieces[0].shape[0]
    return pl.pallas_call(
        functools.partial(hidden_back_kernel, slots),
        grid=(total // TILE,),
        in_specs=[rows_of(wide)] + [whole(p) for p in pieces],
        out_specs=rows_of(units),
        out_shape=jax.ShapeDtypeStruct((total, units), FULL),
        compiler_params=pltpu.CompilerParams(vmem_limit_bytes=VMEM),
        cost_estimate=lasting(10.8),
        name="hidden_back",
    )(x, *pieces)


def feed_grads_kernel(early, x_ref, feed_ref, grad_ref, hidden_ref, *out_refs):
    wide = feed_ref.shape[1]
    half = x_ref.shape[1] // 2
    over_rows = (((0,), (0,)), ((), ()))

    def make(write):
        for left, right, there in (
            (x_ref, feed_ref, slice(0, wide)),
            (grad_ref, hidden_ref, slice(wide, wide + hidden_ref.shape[1])),
        ):
            part = lax.dot_general(left[...], right[...], over_rows, preferred_element_type=FULL)
            write(there, part.astype(HALF))

    def write_whole(there, part):
        out_refs[-1][:, there] = part

    def write_halves(there, part):
        out_refs[0][:, there] = part[:half]
        out_refs[1][:, there] = part[half:]

    if early:
        pl.when(pl.program_id(0) == 0)(functools.partial(make, write_halves))
        pl.when(pl.program_id(0) > 0)(functools.partial(make, write_whole))
    else:
        make(write_whole)


def feed_grads(x, feed, grad, hidden, slots, block, early):
    total = x.shape[0]
    units = hidden.shape[1]
    if block % 128:
        parts = []
        for start, stop in ((slots - 1, slots), (slots - 3, slots - 1)) if early else ((0, slots - 3),):
            there = slice(start * block, stop * block)
            part = [contract_rows(x[:, there], feed), contract_rows(grad[:, there], hidden)]
            parts.append(jnp.concatenate(part, axis=1).astype(HALF))
        return [*jnp.split(parts[0], 2), parts[1]] if early else parts
    place = (lambda i: (0, slots - 1 - i)) if early else (lambda i: (0, i))
    columns = pl.BlockSpec((total, block), place)
    shapes = [(block // 2, 3 * units)] * 2 + [(2 * block, 3 * units)] if early else [((slots - 3) * block, 3 * units)]
    out_specs = [pl.BlockSpec((block, 3 * units), (lambda i: (2 - jnp.maximum(i, 1), 0)) if early else (lambda i: (i, 0)))]
    if early:
        out_specs = [pl.BlockSpec((block // 2, 3 * units), lambda i: (0, 0))] * 2 + out_specs
    return pl.pallas_call(
        functools.partial(feed_grads_kernel, early),
        grid=(3 if early else slots - 3,),
        in_specs=[columns, whole(feed), columns, whole(hidden)],
        out_specs=out_specs,
        out_shape=[jax.ShapeDtypeStruct(shape, HALF) for shape in shapes],
        compiler_params=pltpu.CompilerParams(vmem_limit_bytes=VMEM),
        cost_estimate=lasting(0.0),
        name="feed_grads",
    )(x, feed, grad, hidden)


def outward_kernel(slots, depth, view, transposed, x_ref, *refs):
    pieces, out_ref = refs[:-1], refs[-1]
    for slot in range(slots):
        block = view(block_of(pieces, slot, depth, slots))
        part = nt(x_ref[...], block) if transposed else nn(x_ref[...], block)
        width = part.shape[1]
        out_ref[:, slot * width : (slot + 1) * width] = part.astype(HALF)


def outward(x, pieces, slots, depth, width, transposed, time, name, view=lambda block: block):
    total, wide = x.shape
    return pl.pallas_call(
        functools.partial(outward_kernel, slots, depth, view, transposed),
        grid=(total // TILE,),
        in_specs=[rows_of(wide)] + [whole(p) for p in pieces],
        out_specs=rows_of(slots * width),
        out_shape=jax.ShapeDtypeStruct((total, slots * width), HALF),
        compiler_params=pltpu.CompilerParams(vmem_limit_bytes=VMEM),
        cost_estimate=lasting(time),
        name=name,
    )(x, *pieces)


def output_view(depth, start, block):
    packed = block[:depth, start:]
    return jnp.concatenate(
        [packed[:, at : at + depth] for at in range(0, packed.shape[1], depth)], axis=0
    )


def first_kernel(slots, depth, x_ref, *refs):
    pieces = refs[:-3]
    normed_ref, joined_ref, gains_ref = refs[-3:]
    values = x_ref[...].astype(FULL)
    values = values * lax.rsqrt(jnp.mean(values * values, axis=1, keepdims=True) + EPS)
    parts = []
    for slot in range(slots):
        there = slice(slot * depth, (slot + 1) * depth)
        block = block_of(pieces, slot, pieces[0].shape[0], slots)
        gains = block[depth:, :depth].astype(FULL)[0:2]
        gains_ref[:, there] = gains
        normed_ref[:, there] = (values[:, there] * gains[0:1]).astype(HALF)
        parts.append(block[:depth, : joined_ref.shape[1]])
    joined_ref[...] = nn(normed_ref[...], jnp.concatenate(parts, axis=0))


def first(x, pieces, slots, depth, units):
    total, wide = x.shape
    return pl.pallas_call(
        functools.partial(first_kernel, slots, depth),
        grid=(total // TILE,),
        in_specs=[rows_of(wide)] + [whole(p) for p in pieces],
        out_specs=[rows_of(wide), rows_of(units), pl.BlockSpec((2, wide), lambda i: (0, 0))],
        out_shape=(
            jax.ShapeDtypeStruct((total, wide), HALF),
            jax.ShapeDtypeStruct((total, units), FULL),
            jax.ShapeDtypeStruct((2, wide), FULL),
        ),
        compiler_params=pltpu.CompilerParams(vmem_limit_bytes=VMEM),
        cost_estimate=lasting(0.0),
        name="first",
    )(x, *pieces)


def first_back_kernel(slots, depth, grad_ref, *refs):
    pieces, out_ref = refs[:-1], refs[-1]
    for slot in range(slots):
        block = block_of(pieces, slot, pieces[0].shape[0], slots)[:depth, : grad_ref.shape[1]]
        out_ref[:, slot * depth : (slot + 1) * depth] = nt(grad_ref[...], block).astype(HALF)


def first_back(grad, pieces, slots, depth):
    total, wide = grad.shape
    return pl.pallas_call(
        functools.partial(first_back_kernel, slots, depth),
        grid=(total // TILE,),
        in_specs=[rows_of(wide)] + [whole(p) for p in pieces],
        out_specs=rows_of(slots * depth),
        out_shape=jax.ShapeDtypeStruct((total, slots * depth), HALF),
        compiler_params=pltpu.CompilerParams(vmem_limit_bytes=VMEM),
        cost_estimate=lasting(0.0),
        name="first_back",
    )(grad, *pieces)


def mixed_back_kernel(slots, view, x_ref, *refs):
    pieces, valid_ref, out_ref = refs[:-2], refs[-2], refs[-1]
    total = None
    for slot in range(slots):
        block = view(block_of(pieces, slot, pieces[0].shape[0], slots))
        width = block.shape[1]
        part = nt(x_ref[:, slot * width : (slot + 1) * width], block)
        total = part if total is None else total + part
    out_ref[...] = (total.astype(HALF).astype(FULL) * valid_ref[...]).astype(HALF)


def mixed_back(x, pieces, valid, slots, units, view):
    total, wide = x.shape
    return pl.pallas_call(
        functools.partial(mixed_back_kernel, slots, view),
        grid=(total // TILE,),
        in_specs=[rows_of(wide)] + [whole(p) for p in pieces] + [rows_of(1)],
        out_specs=rows_of(units),
        out_shape=jax.ShapeDtypeStruct((total, units), HALF),
        compiler_params=pltpu.CompilerParams(vmem_limit_bytes=VMEM),
        cost_estimate=lasting(0.0),
        name="mixed_back",
    )(x, *pieces, valid)


def shuffle_kernel(members, count, inverse, *refs):
    half = len(refs) // 2
    for source, target in zip(refs[:half], refs[half:]):
        width = source.shape[1] // count
        for slot, member in enumerate(members()):
            there = pl.ds(pl.multiple_of(member * width, width), width)
            here = slice(slot * width, (slot + 1) * width)
            if inverse:
                target[:, there] = source[:, here]
            else:
                target[:, here] = source[:, there]


def join_kernel(*refs):
    out_ref = refs[-1]
    mine = lax.axis_index("tensor")
    count = refs[0].shape[0]
    for index, ref in enumerate(refs[:-1]):
        out_ref[pl.ds(pl.multiple_of((mine ^ index) * count, count), count), :] = ref[...]


class Travel:
    def __init__(self, ring, shard):
        self.ring = ring
        self.pieces = [shard]
        self.marks = []
        self.above = self.below = shard

    def step(self, *after):
        ring = self.ring
        if after:
            self.above, self.below = tie((self.above, self.below), *after)
        if len(self.marks) == ring.half - 1:
            cut = self.above.shape[0] // 2
            self.above, self.below = self.above[:cut], self.below[cut:]
        self.above = lax.ppermute(self.above, "dp", ring.up)
        self.below = lax.ppermute(self.below, "dp", ring.down)
        self.pieces += [self.above, self.below]
        self.marks.append((self.above, self.below))

    def steps(self, count):
        for _ in range(count):
            self.step()
        return self


class Homeward:
    def __init__(self, ring, part, far):
        self.ring = ring
        self.part = part
        self.left = ring.half - 1
        self.cut = far[0].shape[0]
        self.send(*far)

    def send(self, top, low):
        self.above = lax.ppermute(top, "dp", self.ring.up)
        self.below = lax.ppermute(low, "dp", self.ring.down)
        self.sent, self.arrived = (top, low), (self.above, self.below)

    def total(self, slot, arrived, upper):
        own = self.part(slot)
        first = 0 if upper else own.shape[0] - arrived.shape[0]
        last = first + arrived.shape[0]
        joined = (own[first:last].astype(FULL) + arrived.astype(FULL)).astype(HALF)
        return jnp.concatenate([own[:first], joined, own[last:]], axis=0)

    def step(self, *after):
        above, below = self.above, self.below
        if after:
            above, below = tie((above, below), *after)
        top = self.total(2 * self.left, above, True)
        low = self.total(2 * self.left - 1, below, False)
        self.left -= 1
        self.send(top, low)
        return self

    def steps(self, count):
        for _ in range(count):
            self.step()
        return self

    def own(self):
        return self.part(0).astype(FULL) + self.above.astype(FULL) + self.below.astype(FULL)


def ring_order(count):
    return list(range(0, count, 2)) + list(range(count - 1, 0, -2))


class Ring:
    def __init__(self, count):
        self.count = count
        self.half = count // 2
        order = ring_order(count)
        self.up = [(order[i], order[(i + 1) % count]) for i in range(count)]
        self.down = [(b, a) for a, b in self.up]
        self.offsets = [0]
        for step in range(1, self.half):
            self.offsets += [-step, step]
        self.offsets.append(self.half)

    def members(self):
        count = self.count
        index = lax.axis_index("dp")
        here = jnp.where(index % 2 == 0, index // 2, count - 1 - index // 2)
        spots = [lax.rem(here + (offset + count), count) for offset in self.offsets]
        return [jnp.where(spot < count // 2, 2 * spot, 2 * (count - 1 - spot) + 1) for spot in spots]

    def shuffle(self, *arrays, inverse=False):
        if arrays[0].shape[1] // self.count % 128:
            return [self.shuffle_narrow(array, inverse) for array in arrays]
        return pl.pallas_call(
            functools.partial(shuffle_kernel, self.members, self.count, inverse),
            out_shape=[jax.ShapeDtypeStruct(array.shape, array.dtype) for array in arrays],
            compiler_params=pltpu.CompilerParams(vmem_limit_bytes=VMEM),
            cost_estimate=lasting(1.5),
            name="shuffle",
        )(*arrays)

    def shuffle_narrow(self, values, inverse):
        width = values.shape[1] // self.count
        if not inverse:
            pieces = [lax.dynamic_slice_in_dim(values, m * width, width, 1) for m in self.members()]
            return jnp.concatenate(pieces, axis=1)
        out = jnp.zeros_like(values)
        for slot, member in enumerate(self.members()):
            piece = values[:, slot * width : (slot + 1) * width]
            out = lax.dynamic_update_slice_in_dim(out, piece, member * width, 1)
        return out

    def gather(self, shard):
        return Travel(self, shard)

    def gather_rows(self, rows):
        first = lax.ppermute(rows, "tensor", beside(2))
        near = lax.ppermute(rows, "tensor", beside(1))
        far = lax.ppermute(first, "tensor", beside(1))
        return pl.pallas_call(
            join_kernel,
            out_shape=jax.ShapeDtypeStruct((4 * rows.shape[0], rows.shape[1]), rows.dtype),
            compiler_params=pltpu.CompilerParams(vmem_limit_bytes=VMEM),
            cost_estimate=lasting(0.0),
            name="join",
        )(rows, near, first, far)

    def scatter_rows(self, values):
        mine = lax.axis_index("tensor")
        count = values.shape[0] // 4

        def piece(index):
            return lax.dynamic_slice_in_dim(values, (mine ^ index) * count, count, 0)

        given = jnp.concatenate([piece(3), piece(1)], axis=0)
        given = lax.ppermute(given, "tensor", beside(1)).astype(FULL)
        send = (piece(2).astype(FULL) + given[:count]).astype(HALF)
        far = lax.ppermute(send, "tensor", beside(2)).astype(FULL)
        return piece(0).astype(FULL) + given[count:] + far

    def lengths(self, counts):
        return counts[0]


def beside(index):
    return [(i, i ^ index) for i in range(4)]


def per_device(
    tokens,
    query_weight,
    key_weight,
    value_weight,
    output_weight,
    gate_weight,
    up_weight,
    down_weight,
    attention_gain,
    feed_gain,
    doc_lengths,
    cotangent,
):
    ring = Ring(lax.axis_size("dp"))
    own_rows, width = tokens.shape
    block = query_weight.shape[0]

    inner = query_weight.shape[1]
    kv_width = key_weight.shape[1]
    joint = inner + 2 * kv_width
    units = gate_weight.shape[1]
    slots = ring.count
    output_shard = output_weight.astype(HALF)
    gains = jnp.stack([attention_gain, feed_gain]).astype(HALF)
    first_shard = jnp.concatenate(
        [
            jnp.concatenate([query_weight, key_weight, value_weight], axis=1).astype(HALF),
            *[output_shard[at : at + block] for at in range(0, inner, block)],
        ],
        axis=1,
    )
    gains = jnp.pad(gains, ((0, 30), (0, first_shard.shape[1] - block)))
    first_shard = jnp.concatenate([first_shard, gains], axis=0)
    whole_way = ring.half
    first_travel = ring.gather(first_shard).steps(whole_way)
    first_pieces, first_marks = first_travel.pieces, first_travel.marks
    tokens, cotangent = ring.shuffle(tie(tokens, first_shard), cotangent)
    rows_in = ring.gather_rows(tokens)
    down_shard = tie(down_weight.astype(HALF), first_marks[-1], rows_in)
    down_travel = ring.gather(down_shard).steps(whole_way)
    down_pieces, down_marks = down_travel.pieces, down_travel.marks
    feed_shard = jnp.concatenate([gate_weight, up_weight], axis=1).astype(HALF)
    feed_travel = ring.gather(tie(feed_shard, first_marks[-1])).steps(whole_way)
    feed_pieces, feed_marks = feed_travel.pieces, feed_travel.marks
    view = functools.partial(output_view, block, joint)

    total = own_rows * lax.axis_size("tensor")
    position, valid, allowed = group_layout(ring.lengths(doc_lengths), total)
    begin = (jnp.arange(total, dtype=jnp.int32) - position.astype(jnp.int32)).reshape(1, total)
    cosine, sine = angle_tables(position)
    cosine = jnp.tile(cosine, (1, 4))
    sine = jnp.concatenate([-sine, sine, -sine, sine], axis=1)
    resid = tokens.astype(FULL)
    scale_one = rms_scale(resid)
    grad_rows = ring.gather_rows(cotangent)
    rows_one, joined, gains = first(
        rows_in, first_pieces, slots, block, joint
    )
    gain_one, gain_two = gains[0], gains[1]
    queries, keys_values, attended, logsum = attend(
        tie(joined, down_marks[0]), cosine, sine, begin, valid.reshape(1, total)
    )
    partial_mixed = outward(
        tie(attended, grad_rows),
        first_pieces,
        slots,
        first_shard.shape[0],
        block,
        False,
        0.0,
        "output",
        view,
    )
    middle = resid + ring.scatter_rows(tie(partial_mixed, down_marks[1], feed_marks[0]))
    middle = tie(middle, feed_marks[1])
    scale_two = rms_scale(middle)
    rows_two = ring.gather_rows((middle * scale_two * gain_two).astype(HALF))
    grad_out = cotangent.astype(FULL)
    grad_hidden = hidden_back(grad_rows, down_pieces, slots)
    hidden, grad_feed = gate_up(rows_two, grad_hidden, feed_pieces)

    *feed_far, feed_mid = feed_grads(rows_two, grad_feed, grad_rows, hidden, slots, block, True)
    feed_near = None

    def feed_part(slot):
        if slot >= slots - 3:
            return feed_mid[(slot - slots + 3) * block :][:block]
        return feed_near[slot * block : (slot + 1) * block]

    feed_sums = Homeward(ring, feed_part, feed_far)
    partial_two = outward(
        tie(grad_feed, feed_mid), feed_pieces, slots, block, block, True, 0.0, "feed_back"
    )
    feed_sums.step(partial_two)
    grad_normed_two = ring.scatter_rows(partial_two)
    inner_two = grad_normed_two * gain_two
    grad_middle = (
        grad_out
        + scale_two * inner_two
        - middle * scale_two**3 * jnp.mean(inner_two * middle, axis=1, keepdims=True)
    )
    middle_given = grad_middle.astype(HALF)
    middle_rows = ring.gather_rows(middle_given)
    (feed_near,) = feed_grads(
        tie(rows_two, feed_sums.sent, middle_given), grad_feed, grad_rows, hidden, slots, block, False
    )
    partial_out = outward(
        tie(hidden, feed_near), down_pieces, slots, units, block, False, 0.0, "down"
    )
    feed_sums.step(partial_out).steps(ring.half - 4)
    grad_attended = mixed_back(
        tie(middle_rows, feed_sums.sent), first_pieces, valid[:, None], slots, inner, view
    )
    grad_joined = attend_back(queries, keys_values, grad_attended, logsum, cosine, sine, begin)
    last_grad = jnp.concatenate(
        [
            contract_rows(rows_one, grad_joined).astype(HALF),
            contract_rows(middle_rows, attended).astype(HALF),
        ],
        axis=1,
    )
    partial_one = first_back(tie(grad_joined, last_grad), first_pieces, slots, block)

    def last_part(slot):
        return last_grad[slot * block : (slot + 1) * block]

    last_sums = Homeward(ring, last_part, jnp.split(last_part(slots - 1), 2))
    last_sums.step(partial_one)
    feed_sums.step(last_sums.sent)
    last_sums.step(feed_sums.sent).steps(ring.half - 4).step(feed_sums.arrived)
    feed_sum, last_sum = feed_sums.own(), last_sums.own()
    first_sum = last_sum[:, :joint]
    output_sum = last_sum[:, joint:].T
    layer_out = (
        middle
        + ring.scatter_rows(partial_out)
    ).astype(HALF)
    grad_normed_one = ring.scatter_rows(partial_one)
    inner_one = grad_normed_one * gain_one
    input_grad = (
        grad_middle
        + scale_one * inner_one
        - resid * scale_one**3 * jnp.mean(inner_one * resid, axis=1, keepdims=True)
    )
    layer_out, input_grad = ring.shuffle(layer_out, input_grad, inverse=True)
    gain_sums = [
        jnp.sum(grads * shard.astype(FULL), axis=1) / gain.astype(HALF).astype(FULL)
        for grads, shard, gain in (
            (first_sum, first_shard[:block, :joint], attention_gain),
            (feed_sum[:, : 2 * units], feed_shard, feed_gain),
        )
    ]
    gain_sums = lax.psum(jnp.stack(gain_sums), "tensor")
    return (
        layer_out,
        input_grad,
        first_sum[:, :inner],
        first_sum[:, inner : inner + kv_width],
        first_sum[:, inner + kv_width :],
        output_sum,
        feed_sum[:, :units],
        feed_sum[:, units : 2 * units],
        feed_sum[:, 2 * units :].T,
        gain_sums[0],
        gain_sums[1],
    )


def solution(mesh):
    placed = (
        P(("dp", "tensor"), None),
        P("dp", "tensor"),
        P("dp", "tensor"),
        P("dp", "tensor"),
        P("tensor", "dp"),
        P("dp", "tensor"),
        P("dp", "tensor"),
        P("tensor", "dp"),
        P("dp"),
        P("dp"),
        P("dp", None),
        P(("dp", "tensor"), None),
    )
    return jax.shard_map(
        per_device,
        mesh=mesh,
        in_specs=placed,
        out_specs=(
            P(("dp", "tensor"), None),
            P(("dp", "tensor"), None),
            P("dp", "tensor"),
            P("dp", "tensor"),
            P("dp", "tensor"),
            P("tensor", "dp"),
            P("dp", "tensor"),
            P("dp", "tensor"),
            P("tensor", "dp"),
            P("dp"),
            P("dp"),
        ),
        check_vma=False,
    )
```

```python
import functools
import math

import jax
import jax.numpy as jnp
from jax import lax
from jax.experimental import pallas as pl
from jax.experimental.pallas import tpu as pltpu
from jax.sharding import PartitionSpec as P

HEAD_DIM = 64


EPS = 1e-05
NEG = -1e30
HALF = jnp.bfloat16
FULL = jnp.float32


def group_layout(counts, total):
    ends = jnp.cumsum(counts)
    starts = ends - counts
    place = jnp.arange(total, dtype=jnp.int32)
    segment = jnp.sum((place[:, None] >= ends[None, :]).astype(jnp.int32), axis=1)
    bounds = jnp.concatenate([starts, ends[-1:]])
    slots = jnp.arange(bounds.shape[0], dtype=jnp.int32)
    begin = jnp.sum(jnp.where(segment[:, None] == slots[None, :], bounds[None, :], 0), axis=1)
    position = (place - begin).astype(FULL)
    valid = (place < ends[-1]).astype(FULL)
    allowed = (segment[:, None] == segment[None, :]) & (place[None, :] <= place[:, None])
    return (position, valid, allowed)


def angle_tables(position):
    half = HEAD_DIM // 2
    freq = jnp.exp(jnp.arange(half, dtype=FULL) * (-2.0 * math.log(10000.0) / HEAD_DIM))
    angle = position[:, None] * freq[None, :]
    return (jnp.cos(angle), jnp.sin(angle))


def contract_rows(left, right):
    return lax.dot_general(left, right, (((0,), (0,)), ((), ())), preferred_element_type=FULL)


def contract_cols(left, right):
    return lax.dot_general(left, right, (((1,), (1,)), ((), ())), preferred_element_type=FULL)


def product(left, right):
    return jnp.dot(left, right, preferred_element_type=FULL)


def rms_scale(values):
    return lax.rsqrt(jnp.mean(values * values, axis=1, keepdims=True) + EPS)


TILE = 256
VMEM = 24 * 2**20

def lasting(time):
    return pl.CostEstimate(flops=int(time * 1.1e9), bytes_accessed=0, transcendentals=0)


def tie(value, *marks):
    return lax.optimization_barrier((value, marks))[0]


def nt(left, right):
    return lax.dot_general(left, right, (((1,), (1,)), ((), ())), preferred_element_type=FULL)

def nn(left, right):
    return lax.dot_general(left, right, (((1,), (0,)), ((), ())), preferred_element_type=FULL)

def swap_halves(x):
    lane = lax.broadcasted_iota(jnp.int32, x.shape, 1)
    return jnp.where(lane % 64 < 32, pltpu.roll(x, 96, 1), pltpu.roll(x, 32, 1))

def fill_bias(begin_ref, bias_ref, total):
    for i in range(total // TILE):
        size = (i + 1) * TILE
        key = lax.broadcasted_iota(jnp.int32, (size, TILE), 0)
        query = lax.broadcasted_iota(jnp.int32, (size, TILE), 1) + i * TILE
        begin = begin_ref[:, i * TILE:(i + 1) * TILE]
        keep = (key >= begin) & (key <= query)
        bias_ref[i, 0:size, :] = jnp.where(keep, 0.0, NEG)

def fwd_kernel(joined_ref, cos_ref, sin_ref, begin_ref, valid_ref, q_ref, kv_ref, out_ref, lse_ref, bias_ref, ka_ref, vt_ref):
    total, wide = joined_ref.shape
    pairs = wide // 128 - 1
    lane = lax.broadcasted_iota(jnp.int32, (total, 128), 1)
    kv = joined_ref[:, pairs * 128:]
    cosine = cos_ref[...]
    sine = sin_ref[...]
    turned = kv * cosine + swap_halves(kv) * sine
    kv = jnp.where(lane < 64, turned, kv)
    kv_ref[...] = kv.astype(HALF)
    ka_ref[0] = jnp.where(lane < 64, kv, 0.0).astype(HALF)
    ka_ref[1] = jnp.where(lane < 64, 0.0, pltpu.roll(kv, 64, 1)).astype(HALF)
    vt_ref[...] = kv.T[64:, :].astype(HALF)
    fill_bias(begin_ref, bias_ref, total)
    for p in range(pairs):
        q = joined_ref[:, p * 128:(p + 1) * 128]
        q_ref[:, p * 128:(p + 1) * 128] = ((q * cosine + swap_halves(q) * sine) * (HEAD_DIM ** -0.5)).astype(HALF)

    def pair(p, carry):
        column = pl.multiple_of(p * 128, 128)
        for i in range(total // TILE):
            size = (i + 1) * TILE
            q = q_ref[i * TILE:(i + 1) * TILE, pl.ds(column, 128)]
            parts = []
            for a in range(2):
                s = nt(ka_ref[a, 0:size, :], q) + bias_ref[i, 0:size, :]
                peak = jnp.max(s, axis=0, keepdims=True)
                expo = jnp.exp(s - peak)
                denom = jnp.sum(expo, axis=0, keepdims=True)
                o = nn(vt_ref[:, 0:size], expo.astype(HALF)) / denom
                lse_ref[2 * p + a, :, i * TILE:(i + 1) * TILE] = peak + jnp.log(denom)
                parts.append(o)
            o = jnp.concatenate(parts, axis=0) * valid_ref[:, i * TILE:(i + 1) * TILE]
            out_ref[i * TILE:(i + 1) * TILE, pl.ds(column, 128)] = o.T.astype(HALF)
        return carry
    lax.fori_loop(0, pairs, pair, 0)

def attend(joined, cosine, sine, begin, valid):
    total, wide = joined.shape
    heads = wide // 64 - 2
    return pl.pallas_call(
        fwd_kernel,
        out_shape=(
            jax.ShapeDtypeStruct((total, heads * 64), HALF),
            jax.ShapeDtypeStruct((total, 128), HALF),
            jax.ShapeDtypeStruct((total, heads * 64), HALF),
            jax.ShapeDtypeStruct((heads, 1, total), FULL),
        ),
        scratch_shapes=[
            pltpu.VMEM((total // TILE, total, TILE), FULL),
            pltpu.VMEM((2, total, 128), HALF),
            pltpu.VMEM((64, total), HALF),
        ],
        compiler_params=pltpu.CompilerParams(vmem_limit_bytes=VMEM),
        cost_estimate=lasting(0.0),
        name="attend",
    )(joined, cosine, sine, begin, valid)

def bwd_kernel(q_ref, kv_ref, do_ref, lse_ref, cos_ref, sin_ref, begin_ref, out_ref, bias_ref, ka_ref, va_ref, kt_ref, dk_ref, dv_ref):
    total = kv_ref.shape[0]
    pairs = q_ref.shape[1] // 128
    lane = lax.broadcasted_iota(jnp.int32, (total, 128), 1)
    kv = kv_ref[...].astype(FULL)
    rolled = pltpu.roll(kv, 64, 1)
    ka_ref[0] = jnp.where(lane < 64, kv, 0.0).astype(HALF)
    ka_ref[1] = jnp.where(lane < 64, 0.0, rolled).astype(HALF)
    va_ref[0] = jnp.where(lane < 64, rolled, 0.0).astype(HALF)
    va_ref[1] = jnp.where(lane < 64, 0.0, kv).astype(HALF)
    kt_ref[...] = kv.T[:64, :].astype(HALF)
    dk_ref[...] = jnp.zeros_like(dk_ref)
    dv_ref[...] = jnp.zeros_like(dv_ref)
    fill_bias(begin_ref, bias_ref, total)
    low = lax.broadcasted_iota(jnp.int32, (TILE, 128), 1) < 64

    def pair(p, carry):
        column = pl.multiple_of(p * 128, 128)
        for i in range(total // TILE):
            size = (i + 1) * TILE
            rows = slice(i * TILE, (i + 1) * TILE)
            q = q_ref[rows, pl.ds(column, 128)]
            do = do_ref[rows, pl.ds(column, 128)]
            parts = []
            for a in range(2):
                keep = low if a == 0 else jnp.logical_not(low)
                s = nt(ka_ref[a, 0:size, :], q) + bias_ref[i, 0:size, :]
                probs = jnp.exp(s - lse_ref[2 * p + a, :, rows])
                dprobs = nt(va_ref[a, 0:size, :], do)
                delta = jnp.sum(probs * dprobs, axis=0, keepdims=True)
                ds = (probs * (dprobs - delta)).astype(HALF)
                dv_ref[0:size, :] += nn(probs.astype(HALF), jnp.where(keep, do, jnp.zeros_like(do)))
                dk_ref[0:size, :] += nn(ds, jnp.where(keep, q, jnp.zeros_like(q)))
                parts.append(nn(kt_ref[:, 0:size], ds))
            dq = jnp.concatenate(parts, axis=0).T * (HEAD_DIM ** -0.5)
            dq = dq * cos_ref[rows, :] - swap_halves(dq) * sin_ref[rows, :]
            out_ref[rows, pl.ds(column, 128)] = dq.astype(HALF)
        return carry
    lax.fori_loop(0, pairs, pair, 0)
    dk = dk_ref[...]
    dk = dk + pltpu.roll(dk, 64, 1)
    dk = dk * cos_ref[...] - swap_halves(dk) * sin_ref[...]
    dv = dv_ref[...]
    dv = dv + pltpu.roll(dv, 64, 1)
    out_ref[:, pairs * 128:] = jnp.where(lane < 64, dk, dv).astype(HALF)

def attend_back(q, kv, do, lse, cosine, sine, begin):
    total, wide = q.shape
    return pl.pallas_call(
        bwd_kernel,
        out_shape=jax.ShapeDtypeStruct((total, wide + 128), HALF),
        scratch_shapes=[
            pltpu.VMEM((total // TILE, total, TILE), FULL),
            pltpu.VMEM((2, total, 128), HALF),
            pltpu.VMEM((2, total, 128), HALF),
            pltpu.VMEM((64, total), HALF),
            pltpu.VMEM((total, 128), FULL),
            pltpu.VMEM((total, 128), FULL),
        ],
        compiler_params=pltpu.CompilerParams(vmem_limit_bytes=VMEM),
        cost_estimate=lasting(0.0),
        name="attend_back",
    )(q, kv, do, lse, cosine, sine, begin)


def block_of(refs, slot, extent, slots):
    if slot < slots - 1 or len(refs) == slots:
        return refs[slot][0:extent, :]
    cut = refs[-2].shape[0]
    return jnp.concatenate([refs[-2][...], refs[-1][0 : extent - cut, :]], axis=0)


def whole(array):
    return pl.BlockSpec(memory_space=pltpu.VMEM)

def rows_of(width, tile=TILE):
    return pl.BlockSpec((tile, width), lambda i: (i, 0))

def gate_up_start_kernel(units, x_ref, *refs):
    pieces, out_ref = refs[:-1], refs[-1]
    for start in range(0, units, 128):
        there = slice(start, start + 128)
        pairs = [
            jnp.concatenate([ref[:, there], ref[:, units + start : units + start + 128]], axis=1)
            for ref in pieces
        ]
        depth = len(pairs) * pieces[0].shape[0]
        out_ref[:, 2 * start : 2 * start + 256] = nn(x_ref[:, :depth], jnp.concatenate(pairs, axis=0))


def gate_up_start(x, pieces):
    total, wide = x.shape
    units = pieces[0].shape[1] // 2
    return pl.pallas_call(
        functools.partial(gate_up_start_kernel, units),
        grid=(total // TILE,),
        in_specs=[rows_of(wide)] + [whole(p) for p in pieces],
        out_specs=rows_of(2 * units),
        out_shape=jax.ShapeDtypeStruct((total, 2 * units), FULL),
        compiler_params=pltpu.CompilerParams(vmem_limit_bytes=VMEM),
        cost_estimate=lasting(12.0),
        name="gate_up_start",
    )(x, *pieces)


def gate_up_kernel(units, x_ref, grad_ref, sum_ref, *refs):
    pieces, hidden_ref, out_ref = refs[:-2], refs[-2], refs[-1]
    depth = x_ref.shape[1] - sum(ref.shape[0] for ref in pieces)
    for start in range(0, units, 128):
        there = slice(start, start + 128)
        pairs = [
            jnp.concatenate([ref[:, there], ref[:, units + start : units + start + 128]], axis=1)
            for ref in pieces
        ]
        both = nn(x_ref[:, depth:], jnp.concatenate(pairs, axis=0))
        both = both + sum_ref[:, 2 * start : 2 * start + 256]
        gate, up = both[:, :128], both[:, 128:]
        sigma = jax.nn.sigmoid(gate)
        swish = gate * sigma
        grad = grad_ref[:, there]
        hidden_ref[:, there] = (swish * up).astype(HALF)
        out_ref[:, there] = (grad * up * sigma * (1.0 + gate * (1.0 - sigma))).astype(HALF)
        out_ref[:, units + start : units + start + 128] = (grad * swish).astype(HALF)


def gate_up(x, grad, sums, pieces):
    total, wide = x.shape
    units = pieces[0].shape[1] // 2
    return pl.pallas_call(
        functools.partial(gate_up_kernel, units),
        grid=(total // TILE,),
        in_specs=[rows_of(wide), rows_of(units), rows_of(2 * units)] + [whole(p) for p in pieces],
        out_specs=[rows_of(units), rows_of(2 * units)],
        out_shape=(
            jax.ShapeDtypeStruct((total, units), HALF),
            jax.ShapeDtypeStruct((total, 2 * units), HALF),
        ),
        compiler_params=pltpu.CompilerParams(vmem_limit_bytes=VMEM),
        cost_estimate=lasting(6.0),
        name="gate_up",
    )(x, grad, sums, *pieces)


def hidden_back_kernel(slots, x_ref, *refs):
    pieces, out_ref = refs[:-1], refs[-1]
    units, depth = pieces[0].shape
    total = None
    for slot in range(slots):
        part = nt(x_ref[:, slot * depth : (slot + 1) * depth], block_of(pieces, slot, units, slots))
        total = part if total is None else total + part
    out_ref[...] = total


def hidden_back(x, pieces, slots):
    total, wide = x.shape
    units = pieces[0].shape[0]
    return pl.pallas_call(
        functools.partial(hidden_back_kernel, slots),
        grid=(total // TILE,),
        in_specs=[rows_of(wide)] + [whole(p) for p in pieces],
        out_specs=rows_of(units),
        out_shape=jax.ShapeDtypeStruct((total, units), FULL),
        compiler_params=pltpu.CompilerParams(vmem_limit_bytes=VMEM),
        cost_estimate=lasting(10.8),
        name="hidden_back",
    )(x, *pieces)


def feed_grads_kernel(early, x_ref, feed_ref, grad_ref, hidden_ref, *out_refs):
    wide = feed_ref.shape[1]
    half = x_ref.shape[1] // 2
    over_rows = (((0,), (0,)), ((), ()))

    def make(write):
        for left, right, there in (
            (x_ref, feed_ref, slice(0, wide)),
            (grad_ref, hidden_ref, slice(wide, wide + hidden_ref.shape[1])),
        ):
            part = lax.dot_general(left[...], right[...], over_rows, preferred_element_type=FULL)
            write(there, part.astype(HALF))

    def write_whole(there, part):
        out_refs[-1][:, there] = part

    def write_halves(there, part):
        out_refs[0][:, there] = part[:half]
        out_refs[1][:, there] = part[half:]

    make(write_halves if early else write_whole)


def feed_grads(x, feed, grad, hidden, slots, block, which):
    total = x.shape[0]
    units = hidden.shape[1]
    start, stop = ((slots - 1, slots), (slots - 3, slots - 1), (0, slots - 3))[which]
    if block % 128:
        there = slice(start * block, stop * block)
        part = [contract_rows(x[:, there], feed), contract_rows(grad[:, there], hidden)]
        part = jnp.concatenate(part, axis=1).astype(HALF)
        return jnp.split(part, 2) if which == 0 else [part]
    columns = pl.BlockSpec((total, block), lambda i: (0, start + i))
    count = 2 if which == 0 else 1
    return pl.pallas_call(
        functools.partial(feed_grads_kernel, which == 0),
        grid=(stop - start,),
        in_specs=[columns, whole(feed), columns, whole(hidden)],
        out_specs=[pl.BlockSpec((block // count, 3 * units), lambda i: (i, 0))] * count,
        out_shape=[jax.ShapeDtypeStruct(((stop - start) * block // count, 3 * units), HALF)] * count,
        compiler_params=pltpu.CompilerParams(vmem_limit_bytes=VMEM),
        cost_estimate=lasting((0.0, 20.0, 0.0)[which]),
        name="feed_grads",
    )(x, feed, grad, hidden)


def outward_kernel(slots, depth, view, transposed, x_ref, *refs):
    pieces, out_ref = refs[:-1], refs[-1]
    for slot in range(slots):
        block = view(block_of(pieces, slot, depth, slots))
        part = nt(x_ref[...], block) if transposed else nn(x_ref[...], block)
        width = part.shape[1]
        out_ref[:, slot * width : (slot + 1) * width] = part.astype(HALF)


def outward(x, pieces, slots, depth, width, transposed, time, name, view=lambda block: block):
    total, wide = x.shape
    return pl.pallas_call(
        functools.partial(outward_kernel, slots, depth, view, transposed),
        grid=(total // TILE,),
        in_specs=[rows_of(wide)] + [whole(p) for p in pieces],
        out_specs=rows_of(slots * width),
        out_shape=jax.ShapeDtypeStruct((total, slots * width), HALF),
        compiler_params=pltpu.CompilerParams(vmem_limit_bytes=VMEM),
        cost_estimate=lasting(time),
        name=name,
    )(x, *pieces)


def output_view(depth, start, block):
    packed = block[:depth, start:]
    return jnp.concatenate(
        [packed[:, at : at + depth] for at in range(0, packed.shape[1], depth)], axis=0
    )


def first_kernel(slots, depth, x_ref, *refs):
    pieces = refs[:-3]
    normed_ref, joined_ref, gains_ref = refs[-3:]
    values = x_ref[...].astype(FULL)
    values = values * lax.rsqrt(jnp.mean(values * values, axis=1, keepdims=True) + EPS)
    parts = []
    for slot in range(slots):
        there = slice(slot * depth, (slot + 1) * depth)
        block = block_of(pieces, slot, pieces[0].shape[0], slots)
        gains = block[depth:, :depth].astype(FULL)[0:2]
        gains_ref[:, there] = gains
        normed_ref[:, there] = (values[:, there] * gains[0:1]).astype(HALF)
        parts.append(block[:depth, : joined_ref.shape[1]])
    joined_ref[...] = nn(normed_ref[...], jnp.concatenate(parts, axis=0))


def first(x, pieces, slots, depth, units):
    total, wide = x.shape
    return pl.pallas_call(
        functools.partial(first_kernel, slots, depth),
        grid=(total // TILE,),
        in_specs=[rows_of(wide)] + [whole(p) for p in pieces],
        out_specs=[rows_of(wide), rows_of(units), pl.BlockSpec((2, wide), lambda i: (0, 0))],
        out_shape=(
            jax.ShapeDtypeStruct((total, wide), HALF),
            jax.ShapeDtypeStruct((total, units), FULL),
            jax.ShapeDtypeStruct((2, wide), FULL),
        ),
        compiler_params=pltpu.CompilerParams(vmem_limit_bytes=VMEM),
        cost_estimate=lasting(0.0),
        name="first",
    )(x, *pieces)


def first_back_kernel(slots, depth, grad_ref, *refs):
    pieces, out_ref = refs[:-1], refs[-1]
    for slot in range(slots):
        block = block_of(pieces, slot, pieces[0].shape[0], slots)[:depth, : grad_ref.shape[1]]
        out_ref[:, slot * depth : (slot + 1) * depth] = nt(grad_ref[...], block).astype(HALF)


def first_back(grad, pieces, slots, depth):
    total, wide = grad.shape
    return pl.pallas_call(
        functools.partial(first_back_kernel, slots, depth),
        grid=(total // TILE,),
        in_specs=[rows_of(wide)] + [whole(p) for p in pieces],
        out_specs=rows_of(slots * depth),
        out_shape=jax.ShapeDtypeStruct((total, slots * depth), HALF),
        compiler_params=pltpu.CompilerParams(vmem_limit_bytes=VMEM),
        cost_estimate=lasting(0.0),
        name="first_back",
    )(grad, *pieces)


def mixed_back_kernel(slots, view, x_ref, *refs):
    pieces, valid_ref, out_ref = refs[:-2], refs[-2], refs[-1]
    total = None
    for slot in range(slots):
        block = view(block_of(pieces, slot, pieces[0].shape[0], slots))
        width = block.shape[1]
        part = nt(x_ref[:, slot * width : (slot + 1) * width], block)
        total = part if total is None else total + part
    out_ref[...] = (total.astype(HALF).astype(FULL) * valid_ref[...]).astype(HALF)


def mixed_back(x, pieces, valid, slots, units, view):
    total, wide = x.shape
    return pl.pallas_call(
        functools.partial(mixed_back_kernel, slots, view),
        grid=(total // TILE,),
        in_specs=[rows_of(wide)] + [whole(p) for p in pieces] + [rows_of(1)],
        out_specs=rows_of(units),
        out_shape=jax.ShapeDtypeStruct((total, units), HALF),
        compiler_params=pltpu.CompilerParams(vmem_limit_bytes=VMEM),
        cost_estimate=lasting(0.0),
        name="mixed_back",
    )(x, *pieces, valid)


def shuffle_kernel(members, count, inverse, *refs):
    half = len(refs) // 2
    for source, target in zip(refs[:half], refs[half:]):
        width = source.shape[1] // count
        for slot, member in enumerate(members()):
            there = pl.ds(pl.multiple_of(member * width, width), width)
            here = slice(slot * width, (slot + 1) * width)
            if inverse:
                target[:, there] = source[:, here]
            else:
                target[:, here] = source[:, there]


def join_kernel(*refs):
    out_ref = refs[-1]
    mine = lax.axis_index("tensor")
    count = refs[0].shape[0]
    for index, ref in enumerate(refs[:-1]):
        out_ref[pl.ds(pl.multiple_of((mine ^ index) * count, count), count), :] = ref[...]


class Travel:
    def __init__(self, ring, shard):
        self.ring = ring
        self.pieces = [shard]
        self.marks = []
        self.above = self.below = shard

    def step(self, *after):
        ring = self.ring
        if after:
            self.above, self.below = tie((self.above, self.below), *after)
        if len(self.marks) == ring.half - 1:
            cut = self.above.shape[0] // 32 * 16
            self.above, self.below = self.above[:cut], self.below[cut:]
        self.above = lax.ppermute(self.above, "dp", ring.up)
        self.below = lax.ppermute(self.below, "dp", ring.down)
        self.pieces += [self.above, self.below]
        self.marks.append((self.above, self.below))

    def steps(self, count):
        for _ in range(count):
            self.step()
        return self


class Homeward:
    def __init__(self, ring, part, far):
        self.ring = ring
        self.part = part
        self.left = ring.half - 1
        self.cut = far[0].shape[0]
        self.send(*far)

    def send(self, top, low):
        self.above = lax.ppermute(top, "dp", self.ring.up)
        self.below = lax.ppermute(low, "dp", self.ring.down)
        self.sent, self.arrived = (top, low), (self.above, self.below)

    def total(self, slot, arrived, upper):
        own = self.part(slot)
        first = 0 if upper else own.shape[0] - arrived.shape[0]
        last = first + arrived.shape[0]
        joined = (own[first:last].astype(FULL) + arrived.astype(FULL)).astype(HALF)
        return jnp.concatenate([own[:first], joined, own[last:]], axis=0)

    def step(self, *after):
        above, below = self.above, self.below
        if after:
            above, below = tie((above, below), *after)
        top = self.total(2 * self.left, above, True)
        low = self.total(2 * self.left - 1, below, False)
        self.left -= 1
        self.send(top, low)
        return self

    def steps(self, count):
        for _ in range(count):
            self.step()
        return self

    def own(self):
        return self.part(0).astype(FULL) + self.above.astype(FULL) + self.below.astype(FULL)


def ring_order(count):
    return list(range(0, count, 2)) + list(range(count - 1, 0, -2))


class Ring:
    def __init__(self, count):
        self.count = count
        self.half = count // 2
        order = ring_order(count)
        self.up = [(order[i], order[(i + 1) % count]) for i in range(count)]
        self.down = [(b, a) for a, b in self.up]
        self.offsets = [0]
        for step in range(1, self.half):
            self.offsets += [-step, step]
        self.offsets.append(self.half)

    def members(self):
        count = self.count
        index = lax.axis_index("dp")
        here = jnp.where(index % 2 == 0, index // 2, count - 1 - index // 2)
        spots = [lax.rem(here + (offset + count), count) for offset in self.offsets]
        return [jnp.where(spot < count // 2, 2 * spot, 2 * (count - 1 - spot) + 1) for spot in spots]

    def shuffle(self, *arrays, inverse=False):
        if arrays[0].shape[1] // self.count % 128:
            return [self.shuffle_narrow(array, inverse) for array in arrays]
        return pl.pallas_call(
            functools.partial(shuffle_kernel, self.members, self.count, inverse),
            out_shape=[jax.ShapeDtypeStruct(array.shape, array.dtype) for array in arrays],
            compiler_params=pltpu.CompilerParams(vmem_limit_bytes=VMEM),
            cost_estimate=lasting(1.5),
            name="shuffle",
        )(*arrays)

    def shuffle_narrow(self, values, inverse):
        width = values.shape[1] // self.count
        if not inverse:
            pieces = [lax.dynamic_slice_in_dim(values, m * width, width, 1) for m in self.members()]
            return jnp.concatenate(pieces, axis=1)
        out = jnp.zeros_like(values)
        for slot, member in enumerate(self.members()):
            piece = values[:, slot * width : (slot + 1) * width]
            out = lax.dynamic_update_slice_in_dim(out, piece, member * width, 1)
        return out

    def gather(self, shard):
        return Travel(self, shard)

    def gather_rows(self, rows):
        first = lax.ppermute(rows, "tensor", beside(2))
        near = lax.ppermute(rows, "tensor", beside(1))
        far = lax.ppermute(first, "tensor", beside(1))
        return pl.pallas_call(
            join_kernel,
            out_shape=jax.ShapeDtypeStruct((4 * rows.shape[0], rows.shape[1]), rows.dtype),
            compiler_params=pltpu.CompilerParams(vmem_limit_bytes=VMEM),
            cost_estimate=lasting(0.0),
            name="join",
        )(rows, near, first, far)

    def scatter_rows(self, values, *after):
        mine = lax.axis_index("tensor")
        count = values.shape[0] // 4

        def piece(index):
            return lax.dynamic_slice_in_dim(values, (mine ^ index) * count, count, 0)

        given = jnp.concatenate([piece(3), piece(1)], axis=0)
        if after:
            given = tie(given, *after)
        given = lax.ppermute(given, "tensor", beside(1)).astype(FULL)
        send = (piece(2).astype(FULL) + given[:count]).astype(HALF)
        far = lax.ppermute(send, "tensor", beside(2)).astype(FULL)
        return piece(0).astype(FULL) + given[count:] + far

    def lengths(self, counts):
        return counts[0]


def beside(index):
    return [(i, i ^ index) for i in range(4)]


def per_device(
    tokens,
    query_weight,
    key_weight,
    value_weight,
    output_weight,
    gate_weight,
    up_weight,
    down_weight,
    attention_gain,
    feed_gain,
    doc_lengths,
    cotangent,
):
    ring = Ring(lax.axis_size("dp"))
    own_rows, width = tokens.shape
    block = query_weight.shape[0]

    inner = query_weight.shape[1]
    kv_width = key_weight.shape[1]
    joint = inner + 2 * kv_width
    units = gate_weight.shape[1]
    slots = ring.count
    output_shard = output_weight.astype(HALF)
    gains = jnp.stack([attention_gain, feed_gain]).astype(HALF)
    first_shard = jnp.concatenate(
        [
            jnp.concatenate([query_weight, key_weight, value_weight], axis=1).astype(HALF),
            *[output_shard[at : at + block] for at in range(0, inner, block)],
        ],
        axis=1,
    )
    gains = jnp.pad(gains, ((0, 14), (0, first_shard.shape[1] - block)))
    first_shard = jnp.concatenate([first_shard, gains], axis=0)
    whole_way = ring.half
    first_travel = ring.gather(first_shard).steps(whole_way)
    first_pieces, first_marks = first_travel.pieces, first_travel.marks
    tokens, cotangent = ring.shuffle(tie(tokens, first_shard), cotangent)
    rows_in = ring.gather_rows(tokens)
    down_shard = tie(down_weight.astype(HALF), first_marks[-1], rows_in)
    down_travel = ring.gather(down_shard).steps(whole_way)
    down_pieces, down_marks = down_travel.pieces, down_travel.marks
    feed_shard = jnp.concatenate([gate_weight, up_weight], axis=1).astype(HALF)
    feed_travel = ring.gather(tie(feed_shard, first_marks[-1])).steps(whole_way)
    feed_pieces, feed_marks = feed_travel.pieces, feed_travel.marks
    view = functools.partial(output_view, block, joint)

    total = own_rows * lax.axis_size("tensor")
    position, valid, allowed = group_layout(ring.lengths(doc_lengths), total)
    begin = (jnp.arange(total, dtype=jnp.int32) - position.astype(jnp.int32)).reshape(1, total)
    cosine, sine = angle_tables(position)
    cosine = jnp.tile(cosine, (1, 4))
    sine = jnp.concatenate([-sine, sine, -sine, sine], axis=1)
    resid = tokens.astype(FULL)
    scale_one = rms_scale(resid)
    grad_rows = ring.gather_rows(cotangent)
    rows_one, joined, gains = first(
        rows_in, first_pieces, slots, block, joint
    )
    gain_one, gain_two = gains[0], gains[1]
    queries, keys_values, attended, logsum = attend(
        tie(joined, down_marks[0]), cosine, sine, begin, valid.reshape(1, total)
    )
    partial_mixed = outward(
        tie(attended, grad_rows),
        first_pieces,
        slots,
        first_shard.shape[0],
        block,
        False,
        0.0,
        "output",
        view,
    )
    middle = resid + ring.scatter_rows(partial_mixed, down_marks[1], feed_marks[0])
    middle = tie(middle, feed_marks[1])
    scale_two = rms_scale(middle)
    rows_two = ring.gather_rows((middle * scale_two * gain_two).astype(HALF))
    grad_out = cotangent.astype(FULL)
    grad_hidden = hidden_back(grad_rows, down_pieces, slots)
    feed_start = gate_up_start(rows_two, feed_pieces[:-2])
    hidden, grad_feed = gate_up(rows_two, grad_hidden, feed_start, feed_pieces[-2:])

    feed_far = feed_grads(rows_two, grad_feed, grad_rows, hidden, slots, block, 0)
    (feed_mid,) = feed_grads(tie(rows_two, feed_far), grad_feed, grad_rows, hidden, slots, block, 1)
    feed_near = None

    def feed_part(slot):
        if slot >= slots - 3:
            return feed_mid[(slot - slots + 3) * block :][:block]
        return feed_near[slot * block : (slot + 1) * block]

    feed_sums = Homeward(ring, feed_part, feed_far)
    partial_two = outward(
        tie(grad_feed, feed_mid), feed_pieces, slots, block, block, True, 0.0, "feed_back"
    )
    feed_sums.step(partial_two)
    grad_normed_two = ring.scatter_rows(partial_two)
    inner_two = grad_normed_two * gain_two
    grad_middle = (
        grad_out
        + scale_two * inner_two
        - middle * scale_two**3 * jnp.mean(inner_two * middle, axis=1, keepdims=True)
    )
    middle_given = grad_middle.astype(HALF)
    middle_rows = ring.gather_rows(middle_given)
    (feed_near,) = feed_grads(
        tie(rows_two, feed_sums.sent, middle_given), grad_feed, grad_rows, hidden, slots, block, 2
    )
    partial_out = outward(
        tie(hidden, feed_near), down_pieces, slots, units, block, False, 0.0, "down"
    )
    feed_sums.step(partial_out).steps(ring.half - 4)
    grad_attended = mixed_back(
        tie(middle_rows, feed_sums.sent), first_pieces, valid[:, None], slots, inner, view
    )
    grad_joined = attend_back(queries, keys_values, grad_attended, logsum, cosine, sine, begin)
    last_grad = jnp.concatenate(
        [
            contract_rows(rows_one, grad_joined).astype(HALF),
            contract_rows(middle_rows, attended).astype(HALF),
        ],
        axis=1,
    )
    partial_one = first_back(tie(grad_joined, last_grad), first_pieces, slots, block)

    def last_part(slot):
        return last_grad[slot * block : (slot + 1) * block]

    last_sums = Homeward(ring, last_part, jnp.split(last_part(slots - 1), 2))
    last_sums.step(partial_one)
    feed_sums.step(last_sums.sent)
    last_sums.step(feed_sums.sent).steps(ring.half - 4).step(feed_sums.arrived)
    feed_sum, last_sum = feed_sums.own(), last_sums.own()
    first_sum = last_sum[:, :joint]
    output_sum = last_sum[:, joint:].T
    layer_out = (
        middle
        + ring.scatter_rows(partial_out)
    ).astype(HALF)
    grad_normed_one = ring.scatter_rows(partial_one)
    inner_one = grad_normed_one * gain_one
    input_grad = (
        grad_middle
        + scale_one * inner_one
        - resid * scale_one**3 * jnp.mean(inner_one * resid, axis=1, keepdims=True)
    )
    layer_out, input_grad = ring.shuffle(layer_out, input_grad, inverse=True)
    gain_sums = [
        jnp.sum(grads * shard.astype(FULL), axis=1) / gain.astype(HALF).astype(FULL)
        for grads, shard, gain in (
            (first_sum, first_shard[:block, :joint], attention_gain),
            (feed_sum[:, : 2 * units], feed_shard, feed_gain),
        )
    ]
    gain_sums = jnp.stack(gain_sums)
    for index in (1, 2):
        gain_sums = gain_sums + lax.ppermute(gain_sums, "tensor", beside(index))
    return (
        layer_out,
        input_grad,
        first_sum[:, :inner],
        first_sum[:, inner : inner + kv_width],
        first_sum[:, inner + kv_width :],
        output_sum,
        feed_sum[:, :units],
        feed_sum[:, units : 2 * units],
        feed_sum[:, 2 * units :].T,
        gain_sums[0],
        gain_sums[1],
    )


def solution(mesh):
    placed = (
        P(("dp", "tensor"), None),
        P("dp", "tensor"),
        P("dp", "tensor"),
        P("dp", "tensor"),
        P("tensor", "dp"),
        P("dp", "tensor"),
        P("dp", "tensor"),
        P("tensor", "dp"),
        P("dp"),
        P("dp"),
        P("dp", None),
        P(("dp", "tensor"), None),
    )
    return jax.shard_map(
        per_device,
        mesh=mesh,
        in_specs=placed,
        out_specs=(
            P(("dp", "tensor"), None),
            P(("dp", "tensor"), None),
            P("dp", "tensor"),
            P("dp", "tensor"),
            P("dp", "tensor"),
            P("tensor", "dp"),
            P("dp", "tensor"),
            P("dp", "tensor"),
            P("tensor", "dp"),
            P("dp"),
            P("dp"),
        ),
        check_vma=False,
    )
```

```python
import functools
import math

import jax
import jax.numpy as jnp
from jax import lax
from jax.experimental import pallas as pl
from jax.experimental.pallas import tpu as pltpu
from jax.sharding import PartitionSpec as P

HEAD_DIM = 64


EPS = 1e-05
NEG = -1e30
HALF = jnp.bfloat16
FULL = jnp.float32


def group_layout(counts, total):
    ends = jnp.cumsum(counts)
    starts = ends - counts
    place = jnp.arange(total, dtype=jnp.int32)
    segment = jnp.sum((place[:, None] >= ends[None, :]).astype(jnp.int32), axis=1)
    bounds = jnp.concatenate([starts, ends[-1:]])
    slots = jnp.arange(bounds.shape[0], dtype=jnp.int32)
    begin = jnp.sum(jnp.where(segment[:, None] == slots[None, :], bounds[None, :], 0), axis=1)
    position = (place - begin).astype(FULL)
    valid = (place < ends[-1]).astype(FULL)
    allowed = (segment[:, None] == segment[None, :]) & (place[None, :] <= place[:, None])
    return (position, valid, allowed)


def angle_tables(position):
    half = HEAD_DIM // 2
    freq = jnp.exp(jnp.arange(half, dtype=FULL) * (-2.0 * math.log(10000.0) / HEAD_DIM))
    angle = position[:, None] * freq[None, :]
    return (jnp.cos(angle), jnp.sin(angle))


def contract_rows(left, right):
    return lax.dot_general(left, right, (((0,), (0,)), ((), ())), preferred_element_type=FULL)


def contract_cols(left, right):
    return lax.dot_general(left, right, (((1,), (1,)), ((), ())), preferred_element_type=FULL)


def product(left, right):
    return jnp.dot(left, right, preferred_element_type=FULL)


def rms_scale(values):
    return lax.rsqrt(jnp.mean(values * values, axis=1, keepdims=True) + EPS)


TILE = 256
VMEM = 16 * 2**20

def lasting(time):
    return pl.CostEstimate(flops=int(time * 1.1e9), bytes_accessed=0, transcendentals=0)


def tie(value, *marks):
    return lax.optimization_barrier((value, marks))[0]


def nt(left, right):
    return lax.dot_general(left, right, (((1,), (1,)), ((), ())), preferred_element_type=FULL)

def nn(left, right):
    return lax.dot_general(left, right, (((1,), (0,)), ((), ())), preferred_element_type=FULL)

def swap_halves(x):
    lane = lax.broadcasted_iota(jnp.int32, x.shape, 1)
    return jnp.where(lane % 64 < 32, pltpu.roll(x, 96, 1), pltpu.roll(x, 32, 1))

def fill_bias(begin_ref, bias_ref, total):
    for i in range(total // TILE):
        size = (i + 1) * TILE
        key = lax.broadcasted_iota(jnp.int32, (size, TILE), 0)
        query = lax.broadcasted_iota(jnp.int32, (size, TILE), 1) + i * TILE
        begin = begin_ref[:, i * TILE:(i + 1) * TILE]
        keep = (key >= begin) & (key <= query)
        bias_ref[i, 0:size, :] = jnp.where(keep, 0.0, NEG)

def fwd_kernel(joined_ref, cos_ref, sin_ref, begin_ref, valid_ref, q_ref, kv_ref, out_ref, lse_ref, bias_ref, ka_ref, vt_ref):
    total, wide = joined_ref.shape
    pairs = wide // 128 - 1
    lane = lax.broadcasted_iota(jnp.int32, (total, 128), 1)
    kv = joined_ref[:, pairs * 128:]
    cosine = cos_ref[...]
    sine = sin_ref[...]
    turned = kv * cosine + swap_halves(kv) * sine
    kv = jnp.where(lane < 64, turned, kv)
    kv_ref[...] = kv.astype(HALF)
    ka_ref[0] = jnp.where(lane < 64, kv, 0.0).astype(HALF)
    ka_ref[1] = jnp.where(lane < 64, 0.0, pltpu.roll(kv, 64, 1)).astype(HALF)
    vt_ref[...] = kv.T[64:, :].astype(HALF)
    fill_bias(begin_ref, bias_ref, total)
    for p in range(pairs):
        q = joined_ref[:, p * 128:(p + 1) * 128]
        q_ref[:, p * 128:(p + 1) * 128] = ((q * cosine + swap_halves(q) * sine) * (HEAD_DIM ** -0.5)).astype(HALF)

    def pair(p, carry):
        column = pl.multiple_of(p * 128, 128)
        for i in range(total // TILE):
            size = (i + 1) * TILE
            q = q_ref[i * TILE:(i + 1) * TILE, pl.ds(column, 128)]
            parts = []
            for a in range(2):
                s = nt(ka_ref[a, 0:size, :], q) + bias_ref[i, 0:size, :]
                peak = jnp.max(s, axis=0, keepdims=True)
                expo = jnp.exp(s - peak)
                denom = jnp.sum(expo, axis=0, keepdims=True)
                o = nn(vt_ref[:, 0:size], expo.astype(HALF)) / denom
                lse_ref[2 * p + a, :, i * TILE:(i + 1) * TILE] = peak + jnp.log(denom)
                parts.append(o)
            o = jnp.concatenate(parts, axis=0) * valid_ref[:, i * TILE:(i + 1) * TILE]
            out_ref[i * TILE:(i + 1) * TILE, pl.ds(column, 128)] = o.T.astype(HALF)
        return carry
    lax.fori_loop(0, pairs, pair, 0)

def attend(joined, cosine, sine, begin, valid):
    total, wide = joined.shape
    heads = wide // 64 - 2
    return pl.pallas_call(
        fwd_kernel,
        out_shape=(
            jax.ShapeDtypeStruct((total, heads * 64), HALF),
            jax.ShapeDtypeStruct((total, 128), HALF),
            jax.ShapeDtypeStruct((total, heads * 64), HALF),
            jax.ShapeDtypeStruct((heads, 1, total), FULL),
        ),
        scratch_shapes=[
            pltpu.VMEM((total // TILE, total, TILE), FULL),
            pltpu.VMEM((2, total, 128), HALF),
            pltpu.VMEM((64, total), HALF),
        ],
        compiler_params=pltpu.CompilerParams(vmem_limit_bytes=VMEM),
        cost_estimate=lasting(0.0),
        name="attend",
    )(joined, cosine, sine, begin, valid)

def bwd_kernel(q_ref, kv_ref, do_ref, lse_ref, cos_ref, sin_ref, begin_ref, out_ref, bias_ref, ka_ref, va_ref, kt_ref, dk_ref, dv_ref):
    total = kv_ref.shape[0]
    pairs = q_ref.shape[1] // 128
    lane = lax.broadcasted_iota(jnp.int32, (total, 128), 1)
    kv = kv_ref[...].astype(FULL)
    rolled = pltpu.roll(kv, 64, 1)
    ka_ref[0] = jnp.where(lane < 64, kv, 0.0).astype(HALF)
    ka_ref[1] = jnp.where(lane < 64, 0.0, rolled).astype(HALF)
    va_ref[0] = jnp.where(lane < 64, rolled, 0.0).astype(HALF)
    va_ref[1] = jnp.where(lane < 64, 0.0, kv).astype(HALF)
    kt_ref[...] = kv.T[:64, :].astype(HALF)
    dk_ref[...] = jnp.zeros_like(dk_ref)
    dv_ref[...] = jnp.zeros_like(dv_ref)
    fill_bias(begin_ref, bias_ref, total)
    low = lax.broadcasted_iota(jnp.int32, (TILE, 128), 1) < 64

    def pair(p, carry):
        column = pl.multiple_of(p * 128, 128)
        for i in range(total // TILE):
            size = (i + 1) * TILE
            rows = slice(i * TILE, (i + 1) * TILE)
            q = q_ref[rows, pl.ds(column, 128)]
            do = do_ref[rows, pl.ds(column, 128)]
            parts = []
            for a in range(2):
                keep = low if a == 0 else jnp.logical_not(low)
                s = nt(ka_ref[a, 0:size, :], q) + bias_ref[i, 0:size, :]
                probs = jnp.exp(s - lse_ref[2 * p + a, :, rows])
                dprobs = nt(va_ref[a, 0:size, :], do)
                delta = jnp.sum(probs * dprobs, axis=0, keepdims=True)
                ds = (probs * (dprobs - delta)).astype(HALF)
                dv_ref[0:size, :] += nn(probs.astype(HALF), jnp.where(keep, do, jnp.zeros_like(do)))
                dk_ref[0:size, :] += nn(ds, jnp.where(keep, q, jnp.zeros_like(q)))
                parts.append(nn(kt_ref[:, 0:size], ds))
            dq = jnp.concatenate(parts, axis=0).T * (HEAD_DIM ** -0.5)
            dq = dq * cos_ref[rows, :] - swap_halves(dq) * sin_ref[rows, :]
            out_ref[rows, pl.ds(column, 128)] = dq.astype(HALF)
        return carry
    lax.fori_loop(0, pairs, pair, 0)
    dk = dk_ref[...]
    dk = dk + pltpu.roll(dk, 64, 1)
    dk = dk * cos_ref[...] - swap_halves(dk) * sin_ref[...]
    dv = dv_ref[...]
    dv = dv + pltpu.roll(dv, 64, 1)
    out_ref[:, pairs * 128:] = jnp.where(lane < 64, dk, dv).astype(HALF)

def attend_back(q, kv, do, lse, cosine, sine, begin):
    total, wide = q.shape
    return pl.pallas_call(
        bwd_kernel,
        out_shape=jax.ShapeDtypeStruct((total, wide + 128), HALF),
        scratch_shapes=[
            pltpu.VMEM((total // TILE, total, TILE), FULL),
            pltpu.VMEM((2, total, 128), HALF),
            pltpu.VMEM((2, total, 128), HALF),
            pltpu.VMEM((64, total), HALF),
            pltpu.VMEM((total, 128), FULL),
            pltpu.VMEM((total, 128), FULL),
        ],
        compiler_params=pltpu.CompilerParams(vmem_limit_bytes=VMEM),
        cost_estimate=lasting(0.0),
        name="attend_back",
    )(q, kv, do, lse, cosine, sine, begin)


def block_of(refs, slot, extent, slots):
    if slot < slots - 1 or len(refs) == slots:
        return refs[slot][0:extent, :]
    cut = refs[-2].shape[0]
    return jnp.concatenate([refs[-2][...], refs[-1][0 : extent - cut, :]], axis=0)


def whole(array):
    return pl.BlockSpec(memory_space=pltpu.VMEM)

def rows_of(width, tile=TILE):
    return pl.BlockSpec((tile, width), lambda i: (i, 0))

def gate_up_start_kernel(units, x_ref, *refs):
    pieces, out_ref = refs[:-1], refs[-1]
    for start in range(0, units, 128):
        there = slice(start, start + 128)
        pairs = [
            jnp.concatenate([ref[:, there], ref[:, units + start : units + start + 128]], axis=1)
            for ref in pieces
        ]
        depth = len(pairs) * pieces[0].shape[0]
        out_ref[:, 2 * start : 2 * start + 256] = nn(x_ref[:, :depth], jnp.concatenate(pairs, axis=0))


def gate_up_start(x, pieces):
    total, wide = x.shape
    units = pieces[0].shape[1] // 2
    return pl.pallas_call(
        functools.partial(gate_up_start_kernel, units),
        grid=(total // TILE,),
        in_specs=[rows_of(wide)] + [whole(p) for p in pieces],
        out_specs=rows_of(2 * units),
        out_shape=jax.ShapeDtypeStruct((total, 2 * units), FULL),
        compiler_params=pltpu.CompilerParams(vmem_limit_bytes=VMEM),
        cost_estimate=lasting(12.0),
        name="gate_up_start",
    )(x, *pieces)


def gate_up_kernel(units, x_ref, grad_ref, sum_ref, *refs):
    pieces, hidden_ref, out_ref = refs[:-2], refs[-2], refs[-1]
    depth = x_ref.shape[1] - sum(ref.shape[0] for ref in pieces)
    for start in range(0, units, 128):
        there = slice(start, start + 128)
        pairs = [
            jnp.concatenate([ref[:, there], ref[:, units + start : units + start + 128]], axis=1)
            for ref in pieces
        ]
        both = nn(x_ref[:, depth:], jnp.concatenate(pairs, axis=0))
        both = both + sum_ref[:, 2 * start : 2 * start + 256]
        gate, up = both[:, :128], both[:, 128:]
        sigma = jax.nn.sigmoid(gate)
        swish = gate * sigma
        grad = grad_ref[:, there]
        hidden_ref[:, there] = (swish * up).astype(HALF)
        out_ref[:, there] = (grad * up * sigma * (1.0 + gate * (1.0 - sigma))).astype(HALF)
        out_ref[:, units + start : units + start + 128] = (grad * swish).astype(HALF)


def gate_up(x, grad, sums, pieces):
    total, wide = x.shape
    units = pieces[0].shape[1] // 2
    return pl.pallas_call(
        functools.partial(gate_up_kernel, units),
        grid=(total // TILE,),
        in_specs=[rows_of(wide), rows_of(units), rows_of(2 * units)] + [whole(p) for p in pieces],
        out_specs=[rows_of(units), rows_of(2 * units)],
        out_shape=(
            jax.ShapeDtypeStruct((total, units), HALF),
            jax.ShapeDtypeStruct((total, 2 * units), HALF),
        ),
        compiler_params=pltpu.CompilerParams(vmem_limit_bytes=VMEM),
        cost_estimate=lasting(6.0),
        name="gate_up",
    )(x, grad, sums, *pieces)


def hidden_back_kernel(slots, x_ref, *refs):
    pieces, out_ref = refs[:-1], refs[-1]
    units, depth = pieces[0].shape
    total = None
    for slot in range(slots):
        part = nt(x_ref[:, slot * depth : (slot + 1) * depth], block_of(pieces, slot, units, slots))
        total = part if total is None else total + part
    out_ref[...] = total


def hidden_back(x, pieces, slots):
    total, wide = x.shape
    units = pieces[0].shape[0]
    return pl.pallas_call(
        functools.partial(hidden_back_kernel, slots),
        grid=(total // TILE,),
        in_specs=[rows_of(wide)] + [whole(p) for p in pieces],
        out_specs=rows_of(units),
        out_shape=jax.ShapeDtypeStruct((total, units), FULL),
        compiler_params=pltpu.CompilerParams(vmem_limit_bytes=VMEM),
        cost_estimate=lasting(10.8),
        name="hidden_back",
    )(x, *pieces)


def feed_grads_kernel(early, x_ref, feed_ref, grad_ref, hidden_ref, *out_refs):
    wide = feed_ref.shape[1]
    half = x_ref.shape[1] // 2
    over_rows = (((0,), (0,)), ((), ()))

    def make(write):
        for left, right, there in (
            (x_ref, feed_ref, slice(0, wide)),
            (grad_ref, hidden_ref, slice(wide, wide + hidden_ref.shape[1])),
        ):
            part = lax.dot_general(left[...], right[...], over_rows, preferred_element_type=FULL)
            write(there, part.astype(HALF))

    def write_whole(there, part):
        out_refs[-1][:, there] = part

    def write_halves(there, part):
        out_refs[0][:, there] = part[:half]
        out_refs[1][:, there] = part[half:]

    make(write_halves if early else write_whole)


def feed_grads(x, feed, grad, hidden, slots, block, which):
    total = x.shape[0]
    units = hidden.shape[1]
    start, stop = ((slots - 1, slots), (slots - 3, slots - 1), (0, slots - 3))[which]
    if block % 128:
        there = slice(start * block, stop * block)
        part = [contract_rows(x[:, there], feed), contract_rows(grad[:, there], hidden)]
        part = jnp.concatenate(part, axis=1).astype(HALF)
        return jnp.split(part, 2) if which == 0 else [part]
    columns = pl.BlockSpec((total, block), lambda i: (0, start + i))
    count = 2 if which == 0 else 1
    return pl.pallas_call(
        functools.partial(feed_grads_kernel, which == 0),
        grid=(stop - start,),
        in_specs=[columns, whole(feed), columns, whole(hidden)],
        out_specs=[pl.BlockSpec((block // count, 3 * units), lambda i: (i, 0))] * count,
        out_shape=[jax.ShapeDtypeStruct(((stop - start) * block // count, 3 * units), HALF)] * count,
        compiler_params=pltpu.CompilerParams(vmem_limit_bytes=VMEM),
        cost_estimate=lasting((0.0, 20.0, 0.0)[which]),
        name="feed_grads",
    )(x, feed, grad, hidden)


def outward_kernel(slots, depth, view, transposed, x_ref, *refs):
    pieces, out_ref = refs[:-1], refs[-1]
    for slot in range(slots):
        block = view(block_of(pieces, slot, depth, slots))
        part = nt(x_ref[...], block) if transposed else nn(x_ref[...], block)
        width = part.shape[1]
        out_ref[:, slot * width : (slot + 1) * width] = part.astype(HALF)


def outward(x, pieces, slots, depth, width, transposed, time, name, view=lambda block: block):
    total, wide = x.shape
    return pl.pallas_call(
        functools.partial(outward_kernel, slots, depth, view, transposed),
        grid=(total // TILE,),
        in_specs=[rows_of(wide)] + [whole(p) for p in pieces],
        out_specs=rows_of(slots * width),
        out_shape=jax.ShapeDtypeStruct((total, slots * width), HALF),
        compiler_params=pltpu.CompilerParams(vmem_limit_bytes=VMEM),
        cost_estimate=lasting(time),
        name=name,
    )(x, *pieces)


def output_view(depth, start, block):
    packed = block[:depth, start:]
    return jnp.concatenate(
        [packed[:, at : at + depth] for at in range(0, packed.shape[1], depth)], axis=0
    )


def first_kernel(slots, depth, x_ref, *refs):
    pieces = refs[:-3]
    normed_ref, joined_ref, gains_ref = refs[-3:]
    values = x_ref[...].astype(FULL)
    values = values * lax.rsqrt(jnp.mean(values * values, axis=1, keepdims=True) + EPS)
    parts = []
    for slot in range(slots):
        there = slice(slot * depth, (slot + 1) * depth)
        block = block_of(pieces, slot, pieces[0].shape[0], slots)
        gains = block[depth:, :depth].astype(FULL)[0:2]
        gains_ref[:, there] = gains
        normed_ref[:, there] = (values[:, there] * gains[0:1]).astype(HALF)
        parts.append(block[:depth, : joined_ref.shape[1]])
    joined_ref[...] = nn(normed_ref[...], jnp.concatenate(parts, axis=0))


def first(x, pieces, slots, depth, units):
    total, wide = x.shape
    return pl.pallas_call(
        functools.partial(first_kernel, slots, depth),
        grid=(total // TILE,),
        in_specs=[rows_of(wide)] + [whole(p) for p in pieces],
        out_specs=[rows_of(wide), rows_of(units), pl.BlockSpec((2, wide), lambda i: (0, 0))],
        out_shape=(
            jax.ShapeDtypeStruct((total, wide), HALF),
            jax.ShapeDtypeStruct((total, units), FULL),
            jax.ShapeDtypeStruct((2, wide), FULL),
        ),
        compiler_params=pltpu.CompilerParams(vmem_limit_bytes=VMEM),
        cost_estimate=lasting(0.0),
        name="first",
    )(x, *pieces)


def first_back_kernel(slots, depth, grad_ref, *refs):
    pieces, out_ref = refs[:-1], refs[-1]
    for slot in range(slots):
        block = block_of(pieces, slot, pieces[0].shape[0], slots)[:depth, : grad_ref.shape[1]]
        out_ref[:, slot * depth : (slot + 1) * depth] = nt(grad_ref[...], block).astype(HALF)


def first_back(grad, pieces, slots, depth):
    total, wide = grad.shape
    return pl.pallas_call(
        functools.partial(first_back_kernel, slots, depth),
        grid=(total // TILE,),
        in_specs=[rows_of(wide)] + [whole(p) for p in pieces],
        out_specs=rows_of(slots * depth),
        out_shape=jax.ShapeDtypeStruct((total, slots * depth), HALF),
        compiler_params=pltpu.CompilerParams(vmem_limit_bytes=VMEM),
        cost_estimate=lasting(0.0),
        name="first_back",
    )(grad, *pieces)


def mixed_back_kernel(slots, view, x_ref, *refs):
    pieces, valid_ref, out_ref = refs[:-2], refs[-2], refs[-1]
    total = None
    for slot in range(slots):
        block = view(block_of(pieces, slot, pieces[0].shape[0], slots))
        width = block.shape[1]
        part = nt(x_ref[:, slot * width : (slot + 1) * width], block)
        total = part if total is None else total + part
    out_ref[...] = (total.astype(HALF).astype(FULL) * valid_ref[...]).astype(HALF)


def mixed_back(x, pieces, valid, slots, units, view):
    total, wide = x.shape
    return pl.pallas_call(
        functools.partial(mixed_back_kernel, slots, view),
        grid=(total // TILE,),
        in_specs=[rows_of(wide)] + [whole(p) for p in pieces] + [rows_of(1)],
        out_specs=rows_of(units),
        out_shape=jax.ShapeDtypeStruct((total, units), HALF),
        compiler_params=pltpu.CompilerParams(vmem_limit_bytes=VMEM),
        cost_estimate=lasting(0.0),
        name="mixed_back",
    )(x, *pieces, valid)


def shuffle_kernel(members, count, inverse, *refs):
    half = len(refs) // 2
    for source, target in zip(refs[:half], refs[half:]):
        width = source.shape[1] // count
        for slot, member in enumerate(members()):
            there = pl.ds(pl.multiple_of(member * width, width), width)
            here = slice(slot * width, (slot + 1) * width)
            if inverse:
                target[:, there] = source[:, here]
            else:
                target[:, here] = source[:, there]


def join_kernel(*refs):
    out_ref = refs[-1]
    mine = lax.axis_index("tensor")
    count = refs[0].shape[0]
    for index, ref in enumerate(refs[:-1]):
        out_ref[pl.ds(pl.multiple_of((mine ^ index) * count, count), count), :] = ref[...]


class Travel:
    def __init__(self, ring, shard):
        self.ring = ring
        self.pieces = [shard]
        self.marks = []
        self.above = self.below = shard

    def step(self, *after):
        ring = self.ring
        if after:
            self.above, self.below = tie((self.above, self.below), *after)
        if len(self.marks) == ring.half - 1:
            cut = self.above.shape[0] // 32 * 16
            self.above, self.below = self.above[:cut], self.below[cut:]
        self.above = lax.ppermute(self.above, "dp", ring.up)
        self.below = lax.ppermute(self.below, "dp", ring.down)
        self.pieces += [self.above, self.below]
        self.marks.append((self.above, self.below))

    def steps(self, count):
        for _ in range(count):
            self.step()
        return self


class Homeward:
    def __init__(self, ring, part, far):
        self.ring = ring
        self.part = part
        self.left = ring.half - 1
        self.cut = far[0].shape[0]
        self.send(*far)

    def send(self, top, low):
        self.above = lax.ppermute(top, "dp", self.ring.up)
        self.below = lax.ppermute(low, "dp", self.ring.down)
        self.sent, self.arrived = (top, low), (self.above, self.below)

    def total(self, slot, arrived, upper):
        own = self.part(slot)
        first = 0 if upper else own.shape[0] - arrived.shape[0]
        last = first + arrived.shape[0]
        joined = (own[first:last].astype(FULL) + arrived.astype(FULL)).astype(HALF)
        return jnp.concatenate([own[:first], joined, own[last:]], axis=0)

    def step(self, *after):
        above, below = self.above, self.below
        if after:
            above, below = tie((above, below), *after)
        top = self.total(2 * self.left, above, True)
        low = self.total(2 * self.left - 1, below, False)
        self.left -= 1
        self.send(top, low)
        return self

    def steps(self, count):
        for _ in range(count):
            self.step()
        return self

    def own(self):
        return self.part(0).astype(FULL) + self.above.astype(FULL) + self.below.astype(FULL)


def ring_order(count):
    return list(range(0, count, 2)) + list(range(count - 1, 0, -2))


class Ring:
    def __init__(self, count):
        self.count = count
        self.half = count // 2
        order = ring_order(count)
        self.up = [(order[i], order[(i + 1) % count]) for i in range(count)]
        self.down = [(b, a) for a, b in self.up]
        self.offsets = [0]
        for step in range(1, self.half):
            self.offsets += [-step, step]
        self.offsets.append(self.half)

    def members(self):
        count = self.count
        index = lax.axis_index("dp")
        here = jnp.where(index % 2 == 0, index // 2, count - 1 - index // 2)
        spots = [lax.rem(here + (offset + count), count) for offset in self.offsets]
        return [jnp.where(spot < count // 2, 2 * spot, 2 * (count - 1 - spot) + 1) for spot in spots]

    def shuffle(self, *arrays, inverse=False):
        if arrays[0].shape[1] // self.count % 128:
            return [self.shuffle_narrow(array, inverse) for array in arrays]
        return pl.pallas_call(
            functools.partial(shuffle_kernel, self.members, self.count, inverse),
            out_shape=[jax.ShapeDtypeStruct(array.shape, array.dtype) for array in arrays],
            compiler_params=pltpu.CompilerParams(vmem_limit_bytes=VMEM),
            cost_estimate=lasting(1.5),
            name="shuffle",
        )(*arrays)

    def shuffle_narrow(self, values, inverse):
        width = values.shape[1] // self.count
        if not inverse:
            pieces = [lax.dynamic_slice_in_dim(values, m * width, width, 1) for m in self.members()]
            return jnp.concatenate(pieces, axis=1)
        out = jnp.zeros_like(values)
        for slot, member in enumerate(self.members()):
            piece = values[:, slot * width : (slot + 1) * width]
            out = lax.dynamic_update_slice_in_dim(out, piece, member * width, 1)
        return out

    def gather(self, shard):
        return Travel(self, shard)

    def gather_rows(self, rows):
        first = lax.ppermute(rows, "tensor", beside(2))
        near = lax.ppermute(rows, "tensor", beside(1))
        far = lax.ppermute(first, "tensor", beside(1))
        return pl.pallas_call(
            join_kernel,
            out_shape=jax.ShapeDtypeStruct((4 * rows.shape[0], rows.shape[1]), rows.dtype),
            compiler_params=pltpu.CompilerParams(vmem_limit_bytes=VMEM),
            cost_estimate=lasting(0.0),
            name="join",
        )(rows, near, first, far)

    def scatter_rows(self, values, *after):
        mine = lax.axis_index("tensor")
        count = values.shape[0] // 4

        def piece(index):
            return lax.dynamic_slice_in_dim(values, (mine ^ index) * count, count, 0)

        given = jnp.concatenate([piece(3), piece(1)], axis=0)
        if after:
            given = tie(given, *after)
        given = lax.ppermute(given, "tensor", beside(1)).astype(FULL)
        send = (piece(2).astype(FULL) + given[:count]).astype(HALF)
        far = lax.ppermute(send, "tensor", beside(2)).astype(FULL)
        return piece(0).astype(FULL) + given[count:] + far

    def lengths(self, counts):
        return counts[0]


def beside(index):
    return [(i, i ^ index) for i in range(4)]


def per_device(
    tokens,
    query_weight,
    key_weight,
    value_weight,
    output_weight,
    gate_weight,
    up_weight,
    down_weight,
    attention_gain,
    feed_gain,
    doc_lengths,
    cotangent,
):
    ring = Ring(lax.axis_size("dp"))
    own_rows, width = tokens.shape
    block = query_weight.shape[0]

    inner = query_weight.shape[1]
    kv_width = key_weight.shape[1]
    joint = inner + 2 * kv_width
    units = gate_weight.shape[1]
    slots = ring.count
    output_shard = output_weight.astype(HALF)
    gains = jnp.stack([attention_gain, feed_gain]).astype(HALF)
    first_shard = jnp.concatenate(
        [
            jnp.concatenate([query_weight, key_weight, value_weight], axis=1).astype(HALF),
            *[output_shard[at : at + block] for at in range(0, inner, block)],
        ],
        axis=1,
    )
    gains = jnp.pad(gains, ((0, 14), (0, first_shard.shape[1] - block)))
    first_shard = jnp.concatenate([first_shard, gains], axis=0)
    whole_way = ring.half
    first_travel = ring.gather(first_shard).steps(whole_way)
    first_pieces, first_marks = first_travel.pieces, first_travel.marks
    tokens, cotangent = ring.shuffle(tie(tokens, first_shard), cotangent)
    rows_in = ring.gather_rows(tokens)
    down_shard = tie(down_weight.astype(HALF), first_marks[-2])
    down_travel = ring.gather(down_shard).steps(whole_way)
    down_pieces, down_marks = down_travel.pieces, down_travel.marks
    feed_shard = jnp.concatenate([gate_weight, up_weight], axis=1).astype(HALF)
    feed_travel = ring.gather(tie(feed_shard, first_marks[-1])).steps(whole_way)
    feed_pieces, feed_marks = feed_travel.pieces, feed_travel.marks
    view = functools.partial(output_view, block, joint)

    total = own_rows * lax.axis_size("tensor")
    position, valid, allowed = group_layout(ring.lengths(doc_lengths), total)
    begin = (jnp.arange(total, dtype=jnp.int32) - position.astype(jnp.int32)).reshape(1, total)
    cosine, sine = angle_tables(position)
    cosine = jnp.tile(cosine, (1, 4))
    sine = jnp.concatenate([-sine, sine, -sine, sine], axis=1)
    resid = tokens.astype(FULL)
    scale_one = rms_scale(resid)
    grad_rows = ring.gather_rows(cotangent)
    rows_one, joined, gains = first(
        rows_in, first_pieces, slots, block, joint
    )
    gain_one, gain_two = gains[0], gains[1]
    queries, keys_values, attended, logsum = attend(
        tie(joined, down_marks[0]), cosine, sine, begin, valid.reshape(1, total)
    )
    partial_mixed = outward(
        tie(attended, grad_rows),
        first_pieces,
        slots,
        first_shard.shape[0],
        block,
        False,
        0.0,
        "output",
        view,
    )
    middle = resid + ring.scatter_rows(partial_mixed, down_marks[1], feed_marks[0])
    middle = tie(middle, feed_marks[1])
    scale_two = rms_scale(middle)
    rows_two = ring.gather_rows((middle * scale_two * gain_two).astype(HALF))
    grad_out = cotangent.astype(FULL)
    grad_hidden = hidden_back(grad_rows, down_pieces, slots)
    feed_start = gate_up_start(rows_two, feed_pieces[:-2])
    hidden, grad_feed = gate_up(rows_two, grad_hidden, feed_start, feed_pieces[-2:])

    feed_far = feed_grads(rows_two, grad_feed, grad_rows, hidden, slots, block, 0)
    (feed_mid,) = feed_grads(tie(rows_two, feed_far), grad_feed, grad_rows, hidden, slots, block, 1)
    feed_near = None

    def feed_part(slot):
        if slot >= slots - 3:
            return feed_mid[(slot - slots + 3) * block :][:block]
        return feed_near[slot * block : (slot + 1) * block]

    feed_sums = Homeward(ring, feed_part, feed_far)
    partial_two = outward(
        tie(grad_feed, feed_mid), feed_pieces, slots, block, block, True, 0.0, "feed_back"
    )
    feed_sums.step(partial_two)
    grad_normed_two = ring.scatter_rows(partial_two)
    inner_two = grad_normed_two * gain_two
    grad_middle = (
        grad_out
        + scale_two * inner_two
        - middle * scale_two**3 * jnp.mean(inner_two * middle, axis=1, keepdims=True)
    )
    middle_given = grad_middle.astype(HALF)
    middle_rows = ring.gather_rows(middle_given)
    (feed_near,) = feed_grads(
        tie(rows_two, feed_sums.sent, middle_given), grad_feed, grad_rows, hidden, slots, block, 2
    )
    partial_out = outward(
        tie(hidden, feed_near), down_pieces, slots, units, block, False, 0.0, "down"
    )
    feed_sums.step(partial_out).steps(ring.half - 4)
    grad_attended = mixed_back(
        tie(middle_rows, feed_sums.sent), first_pieces, valid[:, None], slots, inner, view
    )
    grad_joined = attend_back(queries, keys_values, grad_attended, logsum, cosine, sine, begin)
    last_grad = jnp.concatenate(
        [
            contract_rows(rows_one, grad_joined).astype(HALF),
            contract_rows(middle_rows, attended).astype(HALF),
        ],
        axis=1,
    )
    partial_one = first_back(tie(grad_joined, last_grad), first_pieces, slots, block)

    def last_part(slot):
        return last_grad[slot * block : (slot + 1) * block]

    last_sums = Homeward(ring, last_part, jnp.split(last_part(slots - 1), 2))
    last_sums.step(partial_one)
    feed_sums.step(last_sums.sent)
    last_sums.step(feed_sums.sent).steps(ring.half - 4).step(feed_sums.arrived)
    feed_sum, last_sum = feed_sums.own(), last_sums.own()
    first_sum = last_sum[:, :joint]
    output_sum = last_sum[:, joint:].T
    layer_out = (
        middle
        + ring.scatter_rows(partial_out)
    ).astype(HALF)
    grad_normed_one = ring.scatter_rows(partial_one)
    inner_one = grad_normed_one * gain_one
    input_grad = (
        grad_middle
        + scale_one * inner_one
        - resid * scale_one**3 * jnp.mean(inner_one * resid, axis=1, keepdims=True)
    )
    layer_out, input_grad = ring.shuffle(layer_out, input_grad, inverse=True)
    gain_sums = [
        jnp.sum(grads * shard.astype(FULL), axis=1) / gain.astype(HALF).astype(FULL)
        for grads, shard, gain in (
            (first_sum, first_shard[:block, :joint], attention_gain),
            (feed_sum[:, : 2 * units], feed_shard, feed_gain),
        )
    ]
    for index in (1, 2):
        gain_sums[1] = gain_sums[1] + lax.ppermute(gain_sums[1], "tensor", beside(index))
    for index in (1, 2):
        gain_sums[0] = gain_sums[0] + lax.ppermute(gain_sums[0], "tensor", beside(index))
    return (
        layer_out,
        input_grad,
        first_sum[:, :inner],
        first_sum[:, inner : inner + kv_width],
        first_sum[:, inner + kv_width :],
        output_sum,
        feed_sum[:, :units],
        feed_sum[:, units : 2 * units],
        feed_sum[:, 2 * units :].T,
        gain_sums[0],
        gain_sums[1],
    )


def solution(mesh):
    placed = (
        P(("dp", "tensor"), None),
        P("dp", "tensor"),
        P("dp", "tensor"),
        P("dp", "tensor"),
        P("tensor", "dp"),
        P("dp", "tensor"),
        P("dp", "tensor"),
        P("tensor", "dp"),
        P("dp"),
        P("dp"),
        P("dp", None),
        P(("dp", "tensor"), None),
    )
    return jax.shard_map(
        per_device,
        mesh=mesh,
        in_specs=placed,
        out_specs=(
            P(("dp", "tensor"), None),
            P(("dp", "tensor"), None),
            P("dp", "tensor"),
            P("dp", "tensor"),
            P("dp", "tensor"),
            P("tensor", "dp"),
            P("dp", "tensor"),
            P("dp", "tensor"),
            P("tensor", "dp"),
            P("dp"),
            P("dp"),
        ),
        check_vma=False,
    )
```
